128 devices in a mesh: rows: 8 (over z_lo, x), cols: 16 (over y, z_hi, core).
Axes of the slice: x: 4, y: 4, z: 4 (z_hi: 2, z_lo: 2; z = z_hi * 2 + z_lo), core: 2. Of those that a mesh axis runs over, the one named last changes fastest.
Arguments:
- observed: float32 [32768, 8192], P('rows', 'cols'), may hold values from -8 to 8
- u_start: float32 [32768, 64], P(('rows', 'cols')), may hold values from -3 to 3
- v_start: float32 [8192, 64], P(('cols', 'rows')), may hold values from -3 to 3
Outputs:
- low_rank: float32 [32768, 8192], P('rows', 'cols')
- sparse: float32 [32768, 8192], P('rows', 'cols')
- u_final: float32 [32768, 64], P(('rows', 'cols'))
- v_final: float32 [8192, 64], P(('cols', 'rows'))
The draws below stay inside these ranges and needn't reach their ends.
All inputs are finite; a program needn't handle non-finite values.
Results may differ from the reference program's by a relative error of at most 0.00014.
Values sent between devices are 32-bit elements; how exact they have to be, the bound alone decides.
A program may use at most 128 MiB of HBM per device.

```python
import jax
import jax.numpy as jnp
from jax import lax

RANK = 64
ITERS = 4
NS = 32768
NT = 8192


def block_levels(stream_key, dims, shards, low, high):
    factor_of = 1.0
    for axis_at, blocks in shards:
        draws = jax.random.uniform(jax.random.fold_in(jax.random.fold_in(stream_key, 6), axis_at), (blocks,), jnp.float32, low / len(shards), high / len(shards))
        factor_of = factor_of * jnp.repeat(jnp.exp(draws), dims[axis_at] // blocks).reshape((-1,) + (1,) * (len(dims) - 1 - axis_at))
    return factor_of


def centred(rng, dims, spread, reach, shards=(), kind=jnp.bfloat16):
    drawn = jax.random.normal(rng, dims, jnp.float32) * spread
    if len(shards) > 0:
        drawn = block_levels(rng, dims, shards, -0.22, 0.18) * drawn
    return jnp.clip(drawn, min=-reach, max=reach).astype(kind)


def setup_inputs(seed: int = 0) -> dict:
    key_of = jax.random.split(jax.random.key(seed), 4)
    return {
        "observed": centred(key_of[0], (NS, NT), 1.0, 8.0, ((0, 8), (1, 16)), jnp.float32),
        "u_start": centred(key_of[1], (NS, RANK), 0.35, 3.0, ((0, 128),), jnp.float32),
        "v_start": centred(key_of[2], (NT, RANK), 0.35, 3.0, ((0, 128),), jnp.float32),
    }


SHRINK = 0.5
RIDGE = 1.0
HI = lax.Precision.HIGHEST

def ridge_solve(part, gram):
    eye = jnp.eye(gram.shape[0], dtype=gram.dtype)
    chol = jnp.linalg.cholesky(gram + RIDGE * eye)
    return jax.scipy.linalg.cho_solve((chol, True), part.T).T

def reference(observed, u_start, v_start):
    u_fac = u_start
    v_fac = v_start
    sparse = jnp.zeros_like(observed)
    for step in range(ITERS):
        low = jnp.dot(u_fac, v_fac.T, precision=HI)
        diff = observed - low
        sparse = diff - jnp.clip(diff, -SHRINK, SHRINK)
        remain = observed - sparse
        gram_v = jnp.dot(v_fac.T, v_fac, precision=HI)
        u_fac = ridge_solve(jnp.dot(remain, v_fac, precision=HI), gram_v)
        gram_u = jnp.dot(u_fac.T, u_fac, precision=HI)
        v_fac = ridge_solve(jnp.dot(remain.T, u_fac, precision=HI), gram_u)
    low = jnp.dot(u_fac, v_fac.T, precision=HI)
    return (low, sparse, u_fac, v_fac)
```

```python
import functools

import jax
import jax.numpy as jnp
from jax import lax
from jax.experimental import pallas as pl
from jax.experimental.pallas import tpu as pltpu
from jax.sharding import PartitionSpec as P

ITERS = 4
SHRINK = 0.5
RIDGE = 1.0
RANK = 64
NY = 4
NR = 8
CH = 256
HALF = CH // 2
NT_LOC = 512
NS_LOC = 4096
MESH = pl.DeviceIdType.MESH
HI = lax.Precision.HIGHEST
F32 = jnp.float32
BF16 = jnp.bfloat16


def dot(a, b, dims=((1,), (0,)), precision=None):
    return lax.dot_general(a, b, (dims, ((), ())), precision=precision, preferred_element_type=F32)


def lanes(shape):
    return lax.broadcasted_iota(jnp.int32, shape, len(shape) - 1)


def sublanes(shape):
    return lax.broadcasted_iota(jnp.int32, shape, len(shape) - 2)


def roll64(m):
    return pltpu.roll(m, 64, 1)


def pack_gram(m):
    s = m + roll64(m)
    t = s[:64] + s[64:]
    return jnp.where(lanes((32, 128)) < 64, t[:32], t[32:])


def unpack_gram(k):
    kr = roll64(k)
    left = lanes((32, 128)) < 64
    return jnp.concatenate([jnp.where(left, k, kr), jnp.where(left, kr, k)], axis=0)


def twin_eye():
    return jnp.where((lanes((64, 128)) % 64) == sublanes((64, 128)), 1.0, 0.0).astype(F32)


def ridge_inverse(gg):
    eye = twin_eye()
    left = lanes((64, 128)) < 64
    rows = sublanes((64, 128))
    m = jnp.where(left, gg + RIDGE * eye, eye)
    for k in range(RANK):
        col = jnp.broadcast_to(m[:, k : k + 1], (64, 128))
        prow = m[k : k + 1, :] / col[k : k + 1, :]
        m = jnp.where(rows == k, prow, m - col * prow)
    return jnp.where(left, roll64(m), m)


def apply_weights(inv2):
    zero = jnp.zeros_like(inv2)
    return jnp.concatenate(
        [jnp.concatenate([inv2, zero], axis=1), jnp.concatenate([zero, inv2], axis=1)], axis=0
    )


def split(x):
    hi = x.astype(BF16)
    return hi, (x - hi.astype(F32)).astype(BF16)


def factor_kernel(
    obs_hbm, u0_ref, v0_ref,
    ust, vst, u_out, v_out,
    obs, rh, rl, part, r1, r2, a2, r3, pan, gb, qt2, gu, wl, wr, qs, rq, rg, qp, vn,
    gv1, gv2, gv3, gva,
    obs_sem, s1s, s1r, s2s, s2r, s3s, s3r, azs, azr, ays, ayr, acs, acr,
    g1s, g1r, g2s, g2r, g3s, g3r, qs_s, qs_r, rg_s, rg_r, qa_s, qa_r, v0s, v0r,
):
    row = lax.axis_index("rows")
    col = lax.axis_index("cols")
    y, zh, co = col // 4, (col // 2) % 2, col % 2

    def cid(yy, zz, cc):
        return yy * 4 + zz * 2 + cc

    def pos(cc, yy, zz):
        return cc * 8 + yy * 2 + zz

    sib = {"cols": cid(y, zh, 1 - co)}
    zpeer = {"cols": cid(y, 1 - zh, co)}

    def ypeer(d):
        return {"cols": cid(lax.rem(y + d, NY), zh, co)}

    def rpeer(d):
        return {"rows": lax.rem(row + d, NR)}

    def rcopy(src, dst, ssem, rsem, dev):
        return pltpu.make_async_remote_copy(
            src_ref=src, dst_ref=dst, send_sem=ssem, recv_sem=rsem, device_id=dev, device_id_type=MESH
        )

    load = pltpu.make_async_copy(obs_hbm, obs, obs_sem)
    load.start()

    barrier = pltpu.get_barrier_semaphore()
    peers = [sib, zpeer] + [ypeer(d) for d in range(1, NY)] + [rpeer(d) for d in range(1, NR)]
    for dev in peers:
        pl.semaphore_signal(barrier, inc=1, device_id=dev, device_id_type=MESH)
    pl.semaphore_wait(barrier, len(peers))

    own = pos(co, y, zh)
    left128 = lanes((HALF, 128)) < 64
    left256 = (lanes((HALF, 256)) % 128) < 64

    def apply_chunk(slot, j, buf):
        u2 = dot(pan[slot], gb[...], precision=HI)
        hi, lo = split(u2)
        st = jnp.where(left256, hi.astype(F32), lo.astype(F32)).astype(BF16)
        base = pl.multiple_of(j * CH, CH)
        ust[buf, pl.ds(base, HALF), :] = st[:, :128]
        ust[buf, pl.ds(base + HALF, HALF), :] = st[:, 128:]

    def time_chunk(slot, j, buf):
        apply_chunk(slot, j, buf)
        rows = pl.ds(pl.multiple_of(j * CH, CH), CH)
        us = ust[buf, rows, :]
        ut = us.T
        gu[...] += dot(ut, us)
        qt2[...] += dot(ut, rh[rows, :]) + dot(ut, rl[rows, :])

    def gather_cols(process, buf):
        rcopy(pan.at[own], pan.at[own], azs, azr, zpeer).start()
        for d in range(1, NY):
            rcopy(pan.at[own], pan.at[own], ays.at[d - 1, 0], ayr.at[d - 1, 0], ypeer(d)).start()
        rcopy(pan.at[own], pan.at[own], acs.at[y * 2 + zh], acr.at[y * 2 + zh], sib).start()
        process(own, cid(y, zh, co), buf)
        pz = pos(co, y, 1 - zh)
        rcopy(pan.at[pz], pan.at[pz], azs, azr, zpeer).wait_recv()
        for d in range(1, NY):
            rcopy(pan.at[pz], pan.at[pz], ays.at[d - 1, 1], ayr.at[d - 1, 1], ypeer(d)).start()
        rcopy(pan.at[pz], pan.at[pz], acs.at[y * 2 + 1 - zh], acr.at[y * 2 + 1 - zh], sib).start()
        process(pz, cid(y, 1 - zh, co), buf)

        def from_y(i, carry):
            yy = lax.rem(y + 2 * NY - 1 - i, NY)
            for e in range(2):
                zz = zh if e == 0 else 1 - zh
                p = pos(co, yy, zz)
                rcopy(pan.at[p], pan.at[p], ays.at[i, e], ayr.at[i, e], zpeer).wait_recv()
                rcopy(pan.at[p], pan.at[p], acs.at[yy * 2 + zz], acr.at[yy * 2 + zz], sib).start()
                process(p, cid(yy, zz, co), buf)
            return carry

        lax.fori_loop(0, NY - 1, from_y, 0)

        def from_sib(i, carry):
            yy = lax.rem(y + 2 * NY - i // 2, NY)
            zz = lax.rem(zh + i, 2)
            p = pos(1 - co, yy, zz)
            rcopy(pan.at[p], pan.at[p], acs.at[yy * 2 + zz], acr.at[yy * 2 + zz], sib).wait_recv()
            process(p, cid(yy, zz, 1 - co), buf)
            return carry

        lax.fori_loop(0, 2 * NY, from_sib, 0)
        rcopy(pan.at[own], pan.at[own], azs, azr, zpeer).wait_send()

        def drain_y(i, carry):
            for e in range(2):
                rcopy(pan.at[own], pan.at[own], ays.at[i, e], ayr.at[i, e], zpeer).wait_send()
            return carry

        lax.fori_loop(0, NY - 1, drain_y, 0)

        def drain_sib(i, carry):
            rcopy(pan.at[own], pan.at[own], acs.at[i], acr.at[i], sib).wait_send()
            return carry

        lax.fori_loop(0, 2 * NY, drain_sib, 0)

    def set_time(vt, buf):
        vh, vl = split(vt)
        vst[buf, :, :] = jnp.concatenate([vh, vh, vl, vl], axis=0)
        x = jnp.concatenate([vh.astype(F32), vl.astype(F32)], axis=0).T
        xr = roll64(x)
        left = lanes((NT_LOC, 128)) < 64
        zero = jnp.zeros_like(x)
        wl[...] = jnp.concatenate([jnp.where(left, x, zero), jnp.where(left, xr, zero)], axis=1).astype(BF16)
        wr[...] = jnp.concatenate([jnp.where(left, zero, xr), jnp.where(left, zero, x)], axis=1).astype(BF16)
        pair = jnp.concatenate([vh, vl], axis=0)
        gva[...] = pack_gram(dot(pair, pair, dims=((1,), (1,))))

    def series_chunk(slot, j, buf):
        rows = pl.ds(pl.multiple_of(j * CH, CH), CH)
        us = ust[buf, rows, :]
        low = dot(jnp.concatenate([us, us], axis=1), vst[buf, :, :])
        remain = low + jnp.clip(obs[rows, :] - low, -SHRINK, SHRINK)
        hi, lo = split(remain)
        rh[rows, :] = hi
        rl[rows, :] = lo
        a = dot(jnp.concatenate([hi[:HALF], lo[:HALF]], axis=0), wl[...])
        b = dot(jnp.concatenate([hi[HALF:], lo[HALF:]], axis=0), wr[...])
        s = a + b
        s = s[:, :128] + s[:, 128:]
        part[slot] = s[:HALF] + s[HALF:]

    vn[row] = v0_ref[...]
    for d in range(1, NR):
        rcopy(v0_ref, vn.at[row], v0s.at[d - 1], v0r.at[d - 1], rpeer(d)).start()
    pan[own] = u0_ref[...]
    gb[...] = apply_weights(twin_eye())
    gather_cols(apply_chunk, 0)
    for d in range(1, NR):
        src = lax.rem(row + NR - d, NR)
        rcopy(v0_ref, vn.at[src], v0s.at[d - 1], v0r.at[d - 1], rpeer(d)).wait()
    vt0 = vn[...].reshape(NT_LOC, 128).T
    set_time(vt0[:64], 0)
    load.wait()

    def iteration(t, carry):
        buf = lax.rem(t, 2)
        nxt = 1 - buf
        rcopy(gva, gv1, g1s, g1r, sib).start()

        def to_sib(i, c):
            yy = lax.rem(y + 1 + i, NY)
            for zz in range(2):
                series_chunk(pos(1 - co, yy, zz), cid(yy, zz, 1 - co), buf)
            block = pl.ds(pos(1 - co, yy, 0), 2)
            rcopy(part.at[block], r1.at[pl.ds(yy * 2, 2)], s1s.at[i], s1r.at[i], sib).start()
            return c

        lax.fori_loop(0, NY, to_sib, 0)
        rcopy(gva, gv1, g1s, g1r, sib).wait()
        gva[...] += gv1[...]
        for d in range(1, NY):
            rcopy(gva, gv2.at[d - 1], g2s.at[d - 1], g2r.at[d - 1], ypeer(d)).start()

        def own_core(i):
            yy = lax.rem(y + 1 + i, NY)
            for zz in range(2):
                series_chunk(pos(co, yy, zz), cid(yy, zz, co), buf)
            block = pl.ds(pos(co, yy, 0), 2)
            other = r1.at[pl.ds(yy * 2, 2)]
            rcopy(part.at[block], other, s1s.at[i], s1r.at[i], sib).wait_recv()
            part[block] += other[...]
            return yy, block

        def to_y(i, c):
            yy, block = own_core(i)
            rcopy(part.at[block], r2.at[i], s2s.at[i], s2r.at[i], {"cols": cid(yy, zh, co)}).start()
            return c

        lax.fori_loop(0, NY - 1, to_y, 0)
        _, mine = own_core(NY - 1)

        for d in range(1, NY):
            rcopy(gva, gv2.at[d - 1], g2s.at[d - 1], g2r.at[d - 1], ypeer(d)).wait()
        gva[...] += gv2[0] + gv2[1] + gv2[2]
        rcopy(gva, gv3, g3s, g3r, zpeer).start()

        for i in range(NY - 1):
            rcopy(part.at[mine], r2.at[i], s2s.at[i], s2r.at[i], zpeer).wait_recv()
        a2[...] = part[mine] + r2[0] + r2[1] + r2[2]
        hop = rcopy(a2.at[1 - zh], r3, s3s, s3r, zpeer)
        hop.start()
        rcopy(gva, gv3, g3s, g3r, zpeer).wait()
        inv_v = ridge_inverse(unpack_gram(gva[...] + gv3[...]))
        gb[...] = apply_weights(inv_v)
        hop.wait()
        pan[own] = a2[zh] + r3[...]

        def drain(i, c):
            rcopy(part.at[mine], r1.at[pl.ds(0, 2)], s1s.at[i], s1r.at[i], sib).wait_send()
            return c

        lax.fori_loop(0, NY, drain, 0)
        for i in range(NY - 1):
            rcopy(part.at[mine], r2.at[i], s2s.at[i], s2r.at[i], zpeer).wait_send()

        gu[...] = jnp.zeros_like(gu)
        qt2[...] = jnp.zeros_like(qt2)
        gather_cols(time_chunk, nxt)

        q = qt2[...]
        qs[...] = (q[:64] + q[64:]).reshape(NR, 8, NT_LOC)
        gva[...] = pack_gram(gu[...])
        for d in range(1, NR):
            peer = lax.rem(row + d, NR)
            rcopy(qs.at[peer], rq.at[d - 1], qs_s.at[d - 1], qs_r.at[d - 1], rpeer(d)).start()
            rcopy(gva, rg.at[d - 1], rg_s.at[d - 1], rg_r.at[d - 1], rpeer(d)).start()
        acc = qs[row]
        g = gva[...]
        for d in range(1, NR):
            peer = lax.rem(row + d, NR)
            rcopy(qs.at[peer], rq.at[d - 1], qs_s.at[d - 1], qs_r.at[d - 1], rpeer(d)).wait()
            acc += rq[d - 1]
        for d in range(1, NR):
            rcopy(gva, rg.at[d - 1], rg_s.at[d - 1], rg_r.at[d - 1], rpeer(d)).wait()
            g += rg[d - 1]
        qp[row] = acc
        for d in range(1, NR):
            rcopy(qp.at[row], qp.at[row], qa_s.at[d - 1], qa_r.at[d - 1], rpeer(d)).start()
        inv_u = ridge_inverse(unpack_gram(g))
        for d in range(1, NR):
            src = lax.rem(row + NR - d, NR)
            rcopy(qp.at[row], qp.at[src], qa_s.at[d - 1], qa_r.at[d - 1], rpeer(d)).wait()
        vt = dot(inv_u[:, :64], qp[...].reshape(RANK, NT_LOC), precision=HI)
        vn[...] = jnp.concatenate([vt, vt], axis=0).T.reshape(NR, 64, 128)
        set_time(vt, nxt)
        return carry

    lax.fori_loop(0, ITERS, iteration, 0)

    u2 = dot(pan[own], gb[...], precision=HI)
    u_out[pl.ds(0, HALF), :] = u2[:, :RANK]
    u_out[pl.ds(HALF, HALF), :] = u2[:, 128 : 128 + RANK]
    v_out[...] = vn[row][:, :RANK]


def factors(observed, u2, v2):
    vm = pl.BlockSpec(memory_space=pltpu.VMEM)
    dma = pltpu.SemaphoreType.DMA
    return pl.pallas_call(
        factor_kernel,
        out_shape=(
            jax.ShapeDtypeStruct((2, NS_LOC, 128), BF16),
            jax.ShapeDtypeStruct((2, 256, NT_LOC), BF16),
            jax.ShapeDtypeStruct((CH, RANK), F32),
            jax.ShapeDtypeStruct((64, RANK), F32),
        ),
        in_specs=[pl.BlockSpec(memory_space=pl.ANY), vm, vm],
        out_specs=(vm, vm, vm, vm),
        scratch_shapes=[
            pltpu.VMEM((NS_LOC, NT_LOC), F32),
            pltpu.VMEM((NS_LOC, NT_LOC), BF16),
            pltpu.VMEM((NS_LOC, NT_LOC), BF16),
            pltpu.VMEM((16, HALF, 128), F32),
            pltpu.VMEM((8, HALF, 128), F32),
            pltpu.VMEM((3, 2, HALF, 128), F32),
            pltpu.VMEM((2, HALF, 128), F32),
            pltpu.VMEM((HALF, 128), F32),
            pltpu.VMEM((16, HALF, 128), F32),
            pltpu.VMEM((128, 256), F32),
            pltpu.VMEM((128, NT_LOC), F32),
            pltpu.VMEM((128, 128), F32),
            pltpu.VMEM((NT_LOC, 256), BF16),
            pltpu.VMEM((NT_LOC, 256), BF16),
            pltpu.VMEM((NR, 8, NT_LOC), F32),
            pltpu.VMEM((NR - 1, 8, NT_LOC), F32),
            pltpu.VMEM((NR - 1, 32, 128), F32),
            pltpu.VMEM((NR, 8, NT_LOC), F32),
            pltpu.VMEM((NR, 64, 128), F32),
            pltpu.VMEM((32, 128), F32),
            pltpu.VMEM((3, 32, 128), F32),
            pltpu.VMEM((32, 128), F32),
            pltpu.VMEM((32, 128), F32),
            dma,
            dma((4,)), dma((4,)), dma((3,)), dma((3,)), dma, dma,
            dma, dma, dma((3, 2)), dma((3, 2)), dma((8,)), dma((8,)),
            dma, dma, dma((3,)), dma((3,)), dma, dma,
            dma((7,)), dma((7,)), dma((7,)), dma((7,)), dma((7,)), dma((7,)), dma((7,)), dma((7,)),
        ],
        compiler_params=pltpu.CompilerParams(
            collective_id=0, has_side_effects=True, vmem_limit_bytes=52 * 1024 * 1024
        ),
        name="factor_updates",
    )(observed, u2, v2)


def slabs_kernel(obs_ref, u_ref, v_ref, low_ref, sparse_ref):
    def low(k):
        us = u_ref[k]
        return dot(jnp.concatenate([us, us], axis=1), v_ref[k])

    low_ref[...] = low(0)
    diff = obs_ref[...] - low(1)
    sparse_ref[...] = diff - jnp.clip(diff, -SHRINK, SHRINK)


def slabs(observed, ust, vst):
    block = 512
    wide = pl.BlockSpec((block, NT_LOC), lambda i: (i, 0))
    return pl.pallas_call(
        slabs_kernel,
        grid=(NS_LOC // block,),
        out_shape=(jax.ShapeDtypeStruct((NS_LOC, NT_LOC), F32),) * 2,
        in_specs=[
            wide,
            pl.BlockSpec((2, block, 128), lambda i: (0, i, 0)),
            pl.BlockSpec((2, 256, NT_LOC), lambda i: (0, 0, 0)),
        ],
        out_specs=(wide, wide),
        compiler_params=pltpu.CompilerParams(vmem_limit_bytes=40 * 1024 * 1024),
        name="final_slabs",
    )(observed, ust, vst)


def shards(observed, u_start, v_start):
    u2 = jnp.concatenate([u_start[:HALF], u_start[HALF:]], axis=1)
    v2 = jnp.concatenate([v_start, v_start], axis=1)
    ust, vst, u_own, v_own = factors(observed, u2, v2)
    low, sparse = slabs(observed, ust, vst)
    return (low, sparse, u_own, v_own)


def solution(mesh):
    return jax.shard_map(
        shards,
        mesh=mesh,
        in_specs=(P("rows", "cols"), P(("rows", "cols"), None), P(("cols", "rows"), None)),
        out_specs=(
            P("rows", "cols"),
            P("rows", "cols"),
            P(("rows", "cols"), None),
            P(("cols", "rows"), None),
        ),
        check_vma=False,
    )
```

```python
import functools

import jax
import jax.numpy as jnp
from jax import lax
from jax.experimental import pallas as pl
from jax.experimental.pallas import tpu as pltpu
from jax.sharding import PartitionSpec as P

ITERS = 4
SHRINK = 0.5
RIDGE = 1.0
RANK = 64
NY = 4
NR = 8
CH = 256
HALF = CH // 2
NT_LOC = 512
NS_LOC = 4096
FACTOR_VMEM = 34
SLABS_VMEM = 24
MESH = pl.DeviceIdType.MESH
HI = lax.Precision.HIGHEST
F32 = jnp.float32
BF16 = jnp.bfloat16


def dot(a, b, dims=((1,), (0,)), precision=None):
    return lax.dot_general(a, b, (dims, ((), ())), precision=precision, preferred_element_type=F32)


def lanes(shape):
    return lax.broadcasted_iota(jnp.int32, shape, len(shape) - 1)


def sublanes(shape):
    return lax.broadcasted_iota(jnp.int32, shape, len(shape) - 2)


def roll64(m):
    return pltpu.roll(m, 64, 1)


def pack_gram(m):
    s = m + roll64(m)
    t = s[:64] + s[64:]
    return jnp.where(lanes((32, 128)) < 64, t[:32], t[32:])


def unpack_gram(k):
    kr = roll64(k)
    left = lanes((32, 128)) < 64
    return jnp.concatenate([jnp.where(left, k, kr), jnp.where(left, kr, k)], axis=0)


def twin_eye():
    return jnp.where((lanes((64, 128)) % 64) == sublanes((64, 128)), 1.0, 0.0).astype(F32)


def ridge_inverse(gg):
    eye = twin_eye()
    left = lanes((64, 128)) < 64
    rows = sublanes((64, 128))
    m = jnp.where(left, gg + RIDGE * eye, eye)
    for k in range(RANK):
        col = jnp.broadcast_to(m[:, k : k + 1], (64, 128))
        prow = m[k : k + 1, :] / col[k : k + 1, :]
        m = jnp.where(rows == k, prow, m - col * prow)
    return jnp.where(left, roll64(m), m)


def split(x):
    hi = x.astype(BF16)
    return hi, (x - hi.astype(F32)).astype(BF16)


def split3(x):
    hi, lo = split(x)
    rest = x - hi.astype(F32) - lo.astype(F32)
    return hi, lo, rest.astype(BF16)


def factor_kernel(
    obs_hbm, u0_ref, v0_ref,
    ust, vst, u_out, v_out,
    obs, rh, rl, part, r1, r2, pan, gw, gi, qt2, gu, wl, wr, qs, rq, rg, qp, vn,
    gv1, gv2, gva, gvb, gua,
    obs_sem, s1s, s1r, s2s, s2r, ays, ayr, acs, acr,
    g1s, g1r, g2s, g2r, qs_s, qs_r, rg_s, rg_r, qa_s, qa_r, v0s, v0r,
):
    row = lax.axis_index("rows")
    col = lax.axis_index("cols")
    y, zh, co = col // 4, (col // 2) % 2, col % 2

    def cid(yy, zz, cc):
        return yy * 4 + zz * 2 + cc

    def pos(cc, yy, zz):
        return cc * 8 + yy * 2 + zz

    def to_chip(k):
        return (y + 1 + k // 2) % NY, (zh + 1 + k) % 2

    def from_chip(k):
        return (y + 2 * NY - 1 - k // 2) % NY, (zh + 1 + k) % 2

    sib = {"cols": cid(y, zh, 1 - co)}

    def chip(k):
        yy, zz = to_chip(k)
        return {"cols": cid(yy, zz, co)}

    def rpeer(d):
        return {"rows": lax.rem(row + d, NR)}

    def rcopy(src, dst, ssem, rsem, dev):
        return pltpu.make_async_remote_copy(
            src_ref=src, dst_ref=dst, send_sem=ssem, recv_sem=rsem, device_id=dev, device_id_type=MESH
        )

    load = pltpu.make_async_copy(obs_hbm, obs, obs_sem)
    load.start()

    barrier = pltpu.get_barrier_semaphore()
    peers = [sib] + [chip(k) for k in range(7)] + [rpeer(d) for d in range(1, NR)]
    for dev in peers:
        pl.semaphore_signal(barrier, inc=1, device_id=dev, device_id_type=MESH)
    pl.semaphore_wait(barrier, len(peers))

    own = pos(co, y, zh)
    left256 = (lanes((HALF, 256)) % 128) < 64

    def set_apply(inv2):
        zero = jnp.zeros_like(inv2)
        g = jnp.concatenate(
            [jnp.concatenate([inv2, zero], axis=1), jnp.concatenate([zero, inv2], axis=1)], axis=0
        )
        g1, g2, g3 = split3(g)
        gw[0] = jnp.concatenate([g1, g1], axis=0)
        gw[1] = jnp.concatenate([g2, g2], axis=0)
        gw[2] = jnp.concatenate([g3, g1], axis=0)

    def solved(slot):
        p1, p2, p3 = split3(pan[slot])
        p12 = jnp.concatenate([p1, p2], axis=1)
        p13 = jnp.concatenate([p1, p3], axis=1)
        return dot(p12, gw[0]) + (dot(p12, gw[1]) + dot(p13, gw[2]))

    def apply_chunk(slot, j, buf):
        hi, lo = split(solved(slot))
        st = jnp.where(left256, hi.astype(F32), lo.astype(F32))
        us = jnp.concatenate([st[:, :128], st[:, 128:]], axis=0)
        ust[buf, pl.ds(pl.multiple_of(j * CH, CH), CH), :] = us.astype(BF16)
        return us

    def apply_chunks(chunks, buf):
        for slot, j in chunks:
            apply_chunk(slot, j, buf)

    def time_chunks(chunks, buf):
        left, right, grams = [], [], []
        for slot, j in chunks:
            rows = pl.ds(pl.multiple_of(j * CH, CH), CH)
            us = apply_chunk(slot, j, buf)
            ut = us.T.astype(BF16)
            left += [ut, ut]
            right += [rh[rows, :], rl[rows, :]]
            grams.append(dot(ut, us.astype(BF16)))
        gu[...] += sum(grams)
        qt2[...] += dot(jnp.concatenate(left, axis=1), jnp.concatenate(right, axis=0))

    def gather_cols(process, buf):
        def chunk(k, cc):
            yy, zz = from_chip(k)
            return pos(cc, yy, zz), cid(yy, zz, cc)

        for k in range(7):
            rcopy(pan.at[own], pan.at[own], ays.at[k], ayr.at[k], chip(k)).start()
        rcopy(pan.at[own], pan.at[own], acs.at[7], acr.at[7], sib).start()
        process([(own, cid(y, zh, co))], buf)

        def arrive(k, carry):
            p, j = chunk(k, co)
            rcopy(pan.at[p], pan.at[p], ays.at[k], ayr.at[k], sib).wait_recv()
            rcopy(pan.at[p], pan.at[p], acs.at[k], acr.at[k], sib).start()
            b = (k + 7) % 8
            ps, js = chunk(b, 1 - co)
            rcopy(pan.at[ps], pan.at[ps], acs.at[b], acr.at[b], sib).wait_recv()
            process([(p, j), (ps, js)], buf)
            return carry

        lax.fori_loop(0, 7, arrive, 0)
        ps, js = chunk(6, 1 - co)
        rcopy(pan.at[ps], pan.at[ps], acs.at[6], acr.at[6], sib).wait_recv()
        process([(ps, js)], buf)

        def drain(k, carry):
            rcopy(pan.at[own], pan.at[own], ays.at[k], ayr.at[k], sib).wait_send()
            rcopy(pan.at[own], pan.at[own], acs.at[k], acr.at[k], sib).wait_send()
            return carry

        lax.fori_loop(0, 7, drain, 0)
        rcopy(pan.at[own], pan.at[own], acs.at[7], acr.at[7], sib).wait_send()

    def time_factor():
        return dot(gi[:, :RANK], qp[...].reshape(RANK, NT_LOC), precision=HI)

    def series_chunks(chunks, buf):
        for slot, j in chunks:
            rows = pl.ds(pl.multiple_of(j * CH, CH), CH)
            us = ust[buf, rows, :]
            low = dot(jnp.concatenate([us, us], axis=1), vst[buf, :, :])
            remain = low + jnp.clip(obs[rows, :] - low, -SHRINK, SHRINK)
            hi, lo = split(remain)
            rh[rows, :] = hi
            rl[rows, :] = lo
            a = dot(jnp.concatenate([hi[:HALF], lo[:HALF]], axis=0), wl[...])
            b = dot(jnp.concatenate([hi[HALF:], lo[HALF:]], axis=0), wr[...])
            s = a + b
            s = s[:, :128] + s[:, 128:]
            part[slot] = s[:HALF] + s[HALF:]

    vn[row] = jnp.zeros((64, 128), F32)
    vn[row, :, pl.ds(0, RANK)] = v0_ref[...]
    for d in range(1, NR):
        rcopy(vn.at[row], vn.at[row], v0s.at[d - 1], v0r.at[d - 1], rpeer(d)).start()
    pan[own] = jnp.concatenate([u0_ref[:, :HALF], u0_ref[:, HALF:]], axis=0).T
    set_apply(twin_eye())
    gather_cols(apply_chunks, 0)
    for d in range(1, NR):
        src = lax.rem(row + NR - d, NR)
        rcopy(vn.at[row], vn.at[src], v0s.at[d - 1], v0r.at[d - 1], rpeer(d)).wait()
    qp[...] = vn[...].reshape(NT_LOC, 128).T[:RANK].reshape(NR, 8, NT_LOC)
    gi[...] = twin_eye()
    load.wait()

    def iteration(t, carry):
        buf = lax.rem(t, 2)
        nxt = 1 - buf
        vh, vl = split(time_factor())
        pair = jnp.concatenate([vh, vl], axis=0)
        gva[...] = pack_gram(dot(pair, pair, dims=((1,), (1,))))
        rcopy(gva, gv1, g1s, g1r, sib).start()
        vst[buf, :, :] = jnp.concatenate([vh, vh, vl, vl], axis=0)
        x = pair.astype(F32).T
        xr = roll64(x)
        left = lanes((NT_LOC, 128)) < 64
        zero = jnp.zeros_like(x)
        wl[...] = jnp.concatenate([jnp.where(left, x, zero), jnp.where(left, xr, zero)], axis=1).astype(BF16)
        wr[...] = jnp.concatenate([jnp.where(left, zero, xr), jnp.where(left, zero, x)], axis=1).astype(BF16)

        def two(i, cc):
            out = []
            for e in range(2):
                yy, zz = to_chip(2 * i + e)
                out.append((pos(cc, yy, zz), cid(yy, zz, cc)))
            return out

        def to_sib(i, c):
            chunks = two(i, 1 - co)
            series_chunks(chunks, buf)
            for e in range(2):
                k = 2 * i + e
                rcopy(part.at[chunks[e][0]], r1.at[k], s1s.at[k], s1r.at[k], sib).start()

            @pl.when(i == 1)
            def _():
                rcopy(gva, gv1, g1s, g1r, sib).wait()
                gvb[...] = gva[...] + gv1[...]
                for k in range(7):
                    rcopy(gvb, gv2.at[k], g2s.at[k], g2r.at[k], chip(k)).start()

            return c

        lax.fori_loop(0, NY, to_sib, 0)

        def own_core(i):
            chunks = two(i, co)
            series_chunks(chunks, buf)
            for e in range(2):
                k = 2 * i + e
                slot = chunks[e][0]
                rcopy(part.at[slot], r1.at[k], s1s.at[k], s1r.at[k], sib).wait_recv()
                part[slot] += r1[k]
            return chunks

        def to_owner(i, c):
            chunks = own_core(i)
            for e in range(2):
                k = 2 * i + e
                rcopy(part.at[chunks[e][0]], r2.at[k], s2s.at[k], s2r.at[k], chip(k)).start()
            return c

        lax.fori_loop(0, NY - 1, to_owner, 0)
        chunks = own_core(NY - 1)
        rcopy(part.at[chunks[0][0]], r2.at[6], s2s.at[6], s2r.at[6], chip(6)).start()

        gu[...] = jnp.zeros_like(gu)
        qt2[...] = jnp.zeros_like(qt2)
        g = gvb[...]
        for k in range(7):
            rcopy(gvb, gv2.at[k], g2s.at[k], g2r.at[k], chip(k)).wait()
            g += gv2[k]
        set_apply(ridge_inverse(unpack_gram(g)))

        s = part[own]
        for k in range(7):
            rcopy(part.at[own], r2.at[k], s2s.at[k], s2r.at[k], chip(k)).wait_recv()
            s += r2[k]
        pan[own] = s

        gather_cols(time_chunks, nxt)

        def drain(k, c):
            rcopy(part.at[own], r1.at[k], s1s.at[k], s1r.at[k], sib).wait_send()
            return c

        lax.fori_loop(0, 8, drain, 0)
        for k in range(7):
            rcopy(part.at[own], r2.at[k], s2s.at[k], s2r.at[k], sib).wait_send()

        gua[...] = pack_gram(gu[...])
        for d in range(1, NR):
            rcopy(gua, rg.at[d - 1], rg_s.at[d - 1], rg_r.at[d - 1], rpeer(d)).start()
        q = qt2[...]
        qs[...] = (q[:64] + q[64:]).reshape(NR, 8, NT_LOC)
        for d in range(1, NR):
            peer = lax.rem(row + d, NR)
            rcopy(qs.at[peer], rq.at[d - 1], qs_s.at[d - 1], qs_r.at[d - 1], rpeer(d)).start()
        acc = qs[row]
        g = gua[...]
        for d in range(1, NR):
            rcopy(gua, rg.at[d - 1], rg_s.at[d - 1], rg_r.at[d - 1], rpeer(d)).wait()
            g += rg[d - 1]
        for d in range(1, NR):
            peer = lax.rem(row + d, NR)
            rcopy(qs.at[peer], rq.at[d - 1], qs_s.at[d - 1], qs_r.at[d - 1], rpeer(d)).wait()
            acc += rq[d - 1]
        qp[row] = acc
        for d in range(1, NR):
            rcopy(qp.at[row], qp.at[row], qa_s.at[d - 1], qa_r.at[d - 1], rpeer(d)).start()
        gi[...] = ridge_inverse(unpack_gram(g))
        for d in range(1, NR):
            src = lax.rem(row + NR - d, NR)
            rcopy(qp.at[row], qp.at[src], qa_s.at[d - 1], qa_r.at[d - 1], rpeer(d)).wait()
        return carry

    lax.fori_loop(0, ITERS, iteration, 0)

    u2 = solved(own)
    u_out[:, pl.ds(0, HALF)] = u2[:, :128].T[:RANK]
    u_out[:, pl.ds(HALF, HALF)] = u2[:, 128:].T[:RANK]
    vt = time_factor()
    vh, vl = split(vt)
    vst[ITERS % 2, :, :] = jnp.concatenate([vh, vh, vl, vl], axis=0)
    vn[...] = jnp.concatenate([vt, vt], axis=0).T.reshape(NR, 64, 128)
    v_out[...] = vn[row, :, pl.ds(0, RANK)]


def factors(observed, ut, v):
    vm = pl.BlockSpec(memory_space=pltpu.VMEM)
    dma = pltpu.SemaphoreType.DMA
    return pl.pallas_call(
        factor_kernel,
        out_shape=(
            jax.ShapeDtypeStruct((2, NS_LOC, 128), BF16),
            jax.ShapeDtypeStruct((2, 256, NT_LOC), BF16),
            jax.ShapeDtypeStruct((RANK, CH), F32),
            jax.ShapeDtypeStruct((64, RANK), F32),
        ),
        in_specs=[pl.BlockSpec(memory_space=pltpu.HBM), vm, vm],
        out_specs=(vm, vm, vm, vm),
        scratch_shapes=[
            pltpu.VMEM((NS_LOC, NT_LOC), F32),
            pltpu.VMEM((NS_LOC, NT_LOC), BF16),
            pltpu.VMEM((NS_LOC, NT_LOC), BF16),
            pltpu.VMEM((16, HALF, 128), F32),
            pltpu.VMEM((8, HALF, 128), F32),
            pltpu.VMEM((7, HALF, 128), F32),
            pltpu.VMEM((16, HALF, 128), F32),
            pltpu.VMEM((3, 256, 256), BF16),
            pltpu.VMEM((64, 128), F32),
            pltpu.VMEM((128, NT_LOC), F32),
            pltpu.VMEM((128, 128), F32),
            pltpu.VMEM((NT_LOC, 256), BF16),
            pltpu.VMEM((NT_LOC, 256), BF16),
            pltpu.VMEM((NR, 8, NT_LOC), F32),
            pltpu.VMEM((NR - 1, 8, NT_LOC), F32),
            pltpu.VMEM((NR - 1, 32, 128), F32),
            pltpu.VMEM((NR, 8, NT_LOC), F32),
            pltpu.VMEM((NR, 64, 128), F32),
            pltpu.VMEM((32, 128), F32),
            pltpu.VMEM((7, 32, 128), F32),
            pltpu.VMEM((32, 128), F32),
            pltpu.VMEM((32, 128), F32),
            pltpu.VMEM((32, 128), F32),
            dma,
            dma((8,)), dma((8,)), dma((7,)), dma((7,)), dma((7,)), dma((7,)), dma((8,)), dma((8,)),
            dma, dma, dma((7,)), dma((7,)),
            dma((7,)), dma((7,)), dma((7,)), dma((7,)), dma((7,)), dma((7,)), dma((7,)), dma((7,)),
        ],
        compiler_params=pltpu.CompilerParams(
            collective_id=0, has_side_effects=True, vmem_limit_bytes=FACTOR_VMEM * 1024 * 1024
        ),
        name="factor_updates",
    )(observed, ut, v)


def slabs_kernel(obs_ref, us_ref, vs_ref, u_ref, v_ref, low_ref, sparse_ref, u_out, v_out):
    def low(k):
        us = us_ref[k]
        return dot(jnp.concatenate([us, us], axis=1), vs_ref[k])

    low_ref[...] = low(0)
    diff = obs_ref[...] - low(1)
    sparse_ref[...] = diff - jnp.clip(diff, -SHRINK, SHRINK)
    u_out[...] = u_ref[...]
    v_out[...] = v_ref[...]


def slabs(observed, ust, vst, u, v):
    block = 512
    wide = pl.BlockSpec((block, NT_LOC), lambda i: (i, 0))
    u_spec = pl.BlockSpec((RANK, CH), lambda i: (0, 0))
    v_spec = pl.BlockSpec((64, RANK), lambda i: (0, 0))
    slab = jax.ShapeDtypeStruct((NS_LOC, NT_LOC), F32)
    return pl.pallas_call(
        slabs_kernel,
        grid=(NS_LOC // block,),
        out_shape=(slab, slab, jax.ShapeDtypeStruct((RANK, CH), F32), jax.ShapeDtypeStruct((64, RANK), F32)),
        in_specs=[
            wide,
            pl.BlockSpec((2, block, 128), lambda i: (0, i, 0)),
            pl.BlockSpec((2, 256, NT_LOC), lambda i: (0, 0, 0)),
            u_spec,
            v_spec,
        ],
        out_specs=(wide, wide, u_spec, v_spec),
        compiler_params=pltpu.CompilerParams(vmem_limit_bytes=SLABS_VMEM * 1024 * 1024),
        name="final_slabs",
    )(observed, ust, vst, u, v)


def shards(observed, u_start, v_start):
    ust, vst, ut, v_own = factors(observed, u_start.T, v_start)
    low, sparse, ut, v_own = slabs(observed, ust, vst, ut, v_own)
    return (low, sparse, ut.T, v_own)


def solution(mesh):
    return jax.shard_map(
        shards,
        mesh=mesh,
        in_specs=(P("rows", "cols"), P(("rows", "cols"), None), P(("cols", "rows"), None)),
        out_specs=(
            P("rows", "cols"),
            P("rows", "cols"),
            P(("rows", "cols"), None),
            P(("cols", "rows"), None),
        ),
        check_vma=False,
    )
```

```python
import functools

import jax
import jax.numpy as jnp
from jax import lax
from jax.experimental import pallas as pl
from jax.experimental.pallas import tpu as pltpu
from jax.sharding import PartitionSpec as P

ITERS = 4
SHRINK = 0.5
RIDGE = 1.0
RANK = 64
NY = 4
NR = 8
CH = 256
HALF = CH // 2
SUB = HALF // 2
NT_LOC = 512
NS_LOC = 4096
FACTOR_VMEM = 48
SLABS_VMEM = 16
MESH = pl.DeviceIdType.MESH
HI = lax.Precision.HIGHEST
F32 = jnp.float32
BF16 = jnp.bfloat16


def dot(a, b, dims=((1,), (0,)), precision=None):
    return lax.dot_general(a, b, (dims, ((), ())), precision=precision, preferred_element_type=F32)


def lanes(shape):
    return lax.broadcasted_iota(jnp.int32, shape, len(shape) - 1)


def sublanes(shape):
    return lax.broadcasted_iota(jnp.int32, shape, len(shape) - 2)


def roll64(m):
    return pltpu.roll(m, 64, 1)


def pack_gram(m):
    s = m + roll64(m)
    t = s[:64] + s[64:]
    return jnp.where(lanes((32, 128)) < 64, t[:32], t[32:])


def unpack_gram(k):
    kr = roll64(k)
    left = lanes((32, 128)) < 64
    return jnp.concatenate([jnp.where(left, k, kr), jnp.where(left, kr, k)], axis=0)


def twin_eye():
    return jnp.where((lanes((64, 128)) % 64) == sublanes((64, 128)), 1.0, 0.0).astype(F32)


def ridge_inverse(gg):
    eye = twin_eye()
    left = lanes((64, 128)) < 64
    rows = sublanes((64, 128))
    m = jnp.where(left, gg + RIDGE * eye, eye)
    for k in range(0, RANK, 2):
        c0 = jnp.broadcast_to(m[:, k : k + 1], (64, 128))
        c1 = jnp.broadcast_to(m[:, k + 1 : k + 2], (64, 128))
        r0, r1 = m[k : k + 1, :], m[k + 1 : k + 2, :]
        a, b = c0[k : k + 1, :], c1[k : k + 1, :]
        d, e = c0[k + 1 : k + 2, :], c1[k + 1 : k + 2, :]
        scale = 1.0 / (a * e - b * d)
        n0 = (e * r0 - b * r1) * scale
        n1 = (a * r1 - d * r0) * scale
        m = jnp.where(rows == k, n0, jnp.where(rows == k + 1, n1, m - c0 * n0 - c1 * n1))
    return jnp.where(left, roll64(m), m)


def split(x):
    hi = x.astype(BF16)
    return hi, (x - hi.astype(F32)).astype(BF16)


def split3(x):
    hi, lo = split(x)
    rest = x - hi.astype(F32) - lo.astype(F32)
    return hi, lo, rest.astype(BF16)


def factor_kernel(
    obs_hbm, u0_hbm, v0_hbm,
    ust, vst, u_out, v_out,
    obs, rh, rl, part, r1, r2, pan, gw, gi, qt2, gu, wl, wr, qs, rq, rg, qp, vn,
    gv1, gv2, gva, gvb, gua, u0_ref, v0_ref,
    obs_sem, u0_sem, v0_sem, s1s, s1r, s2s, s2r, ays, ayr, acs, acr,
    g1s, g1r, g2s, g2r, qs_s, qs_r, rg_s, rg_r, qa_s, qa_r, v0s, v0r,
):
    row = lax.axis_index("rows")
    col = lax.axis_index("cols")
    y, zh, co = col // 4, (col // 2) % 2, col % 2

    def cid(yy, zz, cc):
        return yy * 4 + zz * 2 + cc

    def pos(cc, yy, zz):
        return cc * 8 + yy * 2 + zz

    def to_chip(k):
        return (y + 1 + k // 2) % NY, (zh + 1 + k) % 2

    sib = {"cols": cid(y, zh, 1 - co)}

    def chip(k):
        yy, zz = to_chip(k)
        return {"cols": cid(yy, zz, co)}

    def rpeer(d):
        return {"rows": lax.rem(row + d, NR)}

    def rcopy(src, dst, ssem, rsem, dev):
        return pltpu.make_async_remote_copy(
            src_ref=src, dst_ref=dst, send_sem=ssem, recv_sem=rsem, device_id=dev, device_id_type=MESH
        )

    load_u = pltpu.make_async_copy(u0_hbm, u0_ref, u0_sem)
    load_u.start()
    load_v = pltpu.make_async_copy(v0_hbm, v0_ref, v0_sem)
    load_v.start()
    load = pltpu.make_async_copy(obs_hbm, obs, obs_sem)
    load.start()

    barrier = pltpu.get_barrier_semaphore()
    peers = [sib] + [chip(k) for k in range(7)] + [rpeer(d) for d in range(1, NR)]
    for dev in peers:
        pl.semaphore_signal(barrier, inc=1, device_id=dev, device_id_type=MESH)
    pl.semaphore_wait(barrier, len(peers))

    own = pos(co, y, zh)

    def slab_list(cc, h):
        first = [cid(n // 2, n % 2, cc) * CH + h * SUB for n in range(8)]
        return [pl.ds(pl.multiple_of(f + o, SUB), SUB) for o in (0, HALF) for f in first]

    def rows_of(ref, slabs, *lead):
        return jnp.concatenate([ref[(*lead, q, slice(None))] for q in slabs], axis=0)

    def put_rows(ref, slabs, value, *lead):
        for n, q in enumerate(slabs):
            ref[(*lead, q, slice(None))] = value[n * SUB : (n + 1) * SUB]

    def eight(cc):
        return pl.ds(pl.multiple_of(cc * 8, 8), 8)

    def set_apply(inv2):
        zero = jnp.zeros_like(inv2)
        g = jnp.concatenate(
            [jnp.concatenate([inv2, zero], axis=1), jnp.concatenate([zero, inv2], axis=1)], axis=0
        )
        g1, g2, g3 = split3(g)
        gw[0] = jnp.concatenate([g1, g1], axis=0)
        gw[1] = jnp.concatenate([g2, g2], axis=0)
        gw[2] = jnp.concatenate([g3, g1], axis=0)

    def solved(packed):
        p1, p2, p3 = split3(packed)
        p12 = jnp.concatenate([p1, p2], axis=1)
        p13 = jnp.concatenate([p1, p3], axis=1)
        return dot(p12, gw[0]) + (dot(p12, gw[1]) + dot(p13, gw[2]))

    def apply_chunks(cc, h, buf):
        u2 = solved(pan[h, eight(cc)].reshape(8 * SUB, 128))
        hi, lo = split(u2)
        left = (lanes(u2.shape) % 128) < 64
        st = jnp.where(left, hi.astype(F32), lo.astype(F32))
        us = jnp.concatenate([st[:, :128], st[:, 128:]], axis=0)
        slabs = slab_list(cc, h)
        put_rows(ust, slabs, us.astype(BF16), buf)
        return us, slabs

    def time_chunks(cc, h, buf):
        us, slabs = apply_chunks(cc, h, buf)
        ut = us.T.astype(BF16)
        gu[...] += dot(ut, us.astype(BF16))
        right = jnp.concatenate([rows_of(rh, slabs), rows_of(rl, slabs)], axis=0)
        qt2[...] += dot(jnp.concatenate([ut, ut], axis=1), right)

    def wait_recv(dst, rsem):
        rcopy(dst, dst, rsem, rsem, sib).wait_recv()

    def wait_send(src, ssem):
        rcopy(src, src, ssem, ssem, sib).wait_send()

    def gather_start(h):
        mine = pan.at[h, own]
        for k in range(7):
            rcopy(mine, mine, ays.at[h], ayr.at[h, k], chip(k)).start()

    def gather_finish(process, buf):
        def pair(g, cc):
            return pos(cc, (y + NY - g) % NY, 0)

        def half(h, carry):
            wait_recv(pan.at[h, pos(co, y, 1 - zh)], ayr.at[h, 6])
            block = pan.at[h, pl.ds(pair(0, co), 2)]
            rcopy(block, block, acs.at[h], acr.at[h, 0], sib).start()
            for g in range(1, NY):
                for e in range(2):
                    wait_recv(pan.at[h, pair(g, co) + e], ayr.at[h, 2 * (g - 1) + (zh + 1 + e) % 2])
                block = pan.at[h, pl.ds(pair(g, co), 2)]
                rcopy(block, block, acs.at[h], acr.at[h, g], sib).start()
            process(co, h, buf)
            for g in range(NY):
                wait_recv(pan.at[h, pl.ds(pair(g, 1 - co), 2)], acr.at[h, g])
            process(1 - co, h, buf)
            return carry

        lax.fori_loop(0, 2, half, 0)

    def drain_cols():
        for h in range(2):
            wait_send(pan.at[h, pl.ds(0, 7)], ays.at[h])
            wait_send(pan.at[h, pl.ds(0, 8)], acs.at[h])

    def time_factor():
        return dot(gi[:, :RANK], qp[...].reshape(RANK, NT_LOC), precision=HI)

    def series_chunks(cc, h, buf):
        slabs = slab_list(cc, h)
        n = 8 * SUB
        us = rows_of(ust, slabs, buf)
        low = dot(jnp.concatenate([us, us], axis=1), vst[buf, :, :])
        remain = low + jnp.clip(rows_of(obs, slabs) - low, -SHRINK, SHRINK)
        hi, lo = split(remain)
        put_rows(rh, slabs, hi)
        put_rows(rl, slabs, lo)
        a = dot(jnp.concatenate([hi[:n], lo[:n]], axis=0), wl[...])
        b = dot(jnp.concatenate([hi[n:], lo[n:]], axis=0), wr[...])
        s = a + b
        s = s[:, :128] + s[:, 128:]
        part[h, eight(cc)] = (s[:n] + s[n:]).reshape(8, SUB, 128)

    load_v.wait()
    vn[row] = jnp.zeros((64, 128), F32)
    vn[row, :, pl.ds(0, RANK)] = v0_ref[...]
    for d in range(1, NR):
        rcopy(vn.at[row], vn.at[row], v0s, v0r, rpeer(d)).start()
    load_u.wait()
    u0 = jnp.concatenate([u0_ref[:, :HALF], u0_ref[:, HALF:]], axis=0).T
    for h in range(2):
        pan[h, own] = u0[h * SUB : (h + 1) * SUB]
        gather_start(h)
    set_apply(twin_eye())
    gather_finish(apply_chunks, 0)
    drain_cols()
    wait_recv(vn.at[pl.ds(0, NR - 1)], v0r)
    wait_send(vn.at[pl.ds(0, NR - 1)], v0s)
    qp[...] = vn[...].reshape(NT_LOC, 128).T[:RANK].reshape(NR, 8, NT_LOC)
    gi[...] = twin_eye()
    load.wait()

    def iteration(t, carry):
        buf = lax.rem(t, 2)
        nxt = 1 - buf
        vh, vl = split(time_factor())
        pair = jnp.concatenate([vh, vl], axis=0)
        gva[...] = pack_gram(dot(pair, pair, dims=((1,), (1,))))
        rcopy(gva, gv1, g1s, g1r, sib).start()
        vst[buf, :, :] = jnp.concatenate([vh, vh, vl, vl], axis=0)
        x = pair.astype(F32).T
        xr = roll64(x)
        left = lanes((NT_LOC, 128)) < 64
        zero = jnp.zeros_like(x)
        wl[...] = jnp.concatenate([jnp.where(left, x, zero), jnp.where(left, xr, zero)], axis=1).astype(BF16)
        wr[...] = jnp.concatenate([jnp.where(left, zero, xr), jnp.where(left, zero, x)], axis=1).astype(BF16)

        def sums(h, carry):
            series_chunks(1 - co, h, buf)
            rcopy(part.at[h, eight(1 - co)], r1.at[h], s1s.at[h], s1r.at[h], sib).start()

            @pl.when(h == 0)
            def _():
                rcopy(gva, gv1, g1s, g1r, sib).wait()
                gvb[...] = gva[...] + gv1[...]
                for k in range(7):
                    rcopy(gvb, gv2.at[k], g2s, g2r, chip(k)).start()

            series_chunks(co, h, buf)
            wait_recv(r1.at[h], s1r.at[h])
            part[h, eight(co)] += r1[h]
            for k in range(7):
                yy, zz = to_chip(k)
                rcopy(part.at[h, pos(co, yy, zz)], r2.at[h, k], s2s.at[h], s2r.at[h], chip(k)).start()
            return carry

        lax.fori_loop(0, 2, sums, 0)

        def total(h):
            wait_recv(r2.at[h], s2r.at[h])
            pan[h, own] = part[h, own] + jnp.sum(r2[h], axis=0)
            gather_start(h)

        total(0)
        gu[...] = jnp.zeros_like(gu)
        qt2[...] = jnp.zeros_like(qt2)
        wait_recv(gv2, g2r)
        set_apply(ridge_inverse(unpack_gram(gvb[...] + jnp.sum(gv2[...], axis=0))))
        total(1)
        gather_finish(time_chunks, nxt)

        gua[...] = pack_gram(gu[...])
        for d in range(1, NR):
            rcopy(gua, rg.at[d - 1], rg_s, rg_r, rpeer(d)).start()
        q = qt2[...]
        qs[...] = (q[:64] + q[64:]).reshape(NR, 8, NT_LOC)
        for d in range(1, NR):
            peer = lax.rem(row + d, NR)
            rcopy(qs.at[peer], rq.at[d - 1], qs_s, qs_r, rpeer(d)).start()
        drain_cols()
        wait_send(gv2, g2s)
        for h in range(2):
            wait_send(r1.at[h], s1s.at[h])
            wait_send(r2.at[h], s2s.at[h])
        wait_recv(rg, rg_r)
        g = gua[...] + jnp.sum(rg[...], axis=0)
        wait_recv(rq, qs_r)
        qp[row] = qs[row] + jnp.sum(rq[...], axis=0)
        for d in range(1, NR):
            rcopy(qp.at[row], qp.at[row], qa_s, qa_r, rpeer(d)).start()
        gi[...] = ridge_inverse(unpack_gram(g))
        wait_send(rg, rg_s)
        wait_send(rq, qs_s)
        wait_recv(qp.at[pl.ds(0, NR - 1)], qa_r)
        wait_send(qp.at[pl.ds(0, NR - 1)], qa_s)
        return carry

    lax.fori_loop(0, ITERS, iteration, 0)

    u2 = solved(jnp.concatenate([pan[0, own], pan[1, own]], axis=0))
    u_out[:, pl.ds(0, HALF)] = u2[:, :128].T[:RANK]
    u_out[:, pl.ds(HALF, HALF)] = u2[:, 128:].T[:RANK]
    vt = time_factor()
    vh, vl = split(vt)
    vst[ITERS % 2, :, :] = jnp.concatenate([vh, vh, vl, vl], axis=0)
    vn[...] = jnp.concatenate([vt, vt], axis=0).T.reshape(NR, 64, 128)
    v_out[...] = vn[row, :, pl.ds(0, RANK)]


def factors(observed, ut, v):
    vm = pl.BlockSpec(memory_space=pltpu.VMEM)
    dma = pltpu.SemaphoreType.DMA
    return pl.pallas_call(
        factor_kernel,
        out_shape=(
            jax.ShapeDtypeStruct((2, NS_LOC, 128), BF16),
            jax.ShapeDtypeStruct((2, 256, NT_LOC), BF16),
            jax.ShapeDtypeStruct((RANK, CH), F32),
            jax.ShapeDtypeStruct((64, RANK), F32),
        ),
        in_specs=[pl.BlockSpec(memory_space=pl.ANY)] * 3,
        out_specs=(vm, vm, vm, vm),
        scratch_shapes=[
            pltpu.VMEM((NS_LOC, NT_LOC), F32),
            pltpu.VMEM((NS_LOC, NT_LOC), BF16),
            pltpu.VMEM((NS_LOC, NT_LOC), BF16),
            pltpu.VMEM((2, 16, SUB, 128), F32),
            pltpu.VMEM((2, 8, SUB, 128), F32),
            pltpu.VMEM((2, 7, SUB, 128), F32),
            pltpu.VMEM((2, 16, SUB, 128), F32),
            pltpu.VMEM((3, 256, 256), BF16),
            pltpu.VMEM((64, 128), F32),
            pltpu.VMEM((128, NT_LOC), F32),
            pltpu.VMEM((128, 128), F32),
            pltpu.VMEM((NT_LOC, 256), BF16),
            pltpu.VMEM((NT_LOC, 256), BF16),
            pltpu.VMEM((NR, 8, NT_LOC), F32),
            pltpu.VMEM((NR - 1, 8, NT_LOC), F32),
            pltpu.VMEM((NR - 1, 32, 128), F32),
            pltpu.VMEM((NR, 8, NT_LOC), F32),
            pltpu.VMEM((NR, 64, 128), F32),
            pltpu.VMEM((32, 128), F32),
            pltpu.VMEM((7, 32, 128), F32),
            pltpu.VMEM((32, 128), F32),
            pltpu.VMEM((32, 128), F32),
            pltpu.VMEM((32, 128), F32),
            pltpu.VMEM((RANK, CH), F32),
            pltpu.VMEM((64, RANK), F32),
            dma, dma, dma,
            dma((2,)), dma((2,)), dma((2,)), dma((2,)), dma((2,)), dma((2, 7)), dma((2,)), dma((2, 4)),
            dma, dma, dma, dma,
            dma, dma, dma, dma, dma, dma, dma, dma,
        ],
        compiler_params=pltpu.CompilerParams(
            collective_id=0, has_side_effects=True, vmem_limit_bytes=FACTOR_VMEM * 1024 * 1024
        ),
        cost_estimate=pl.CostEstimate(flops=13_000_000_000, bytes_accessed=12_000_000, transcendentals=0),
        name="factor_updates",
    )(observed, ut, v)


def slabs_kernel(obs_ref, us_ref, vs_ref, u_ref, v_ref, low_ref, sparse_ref, u_out, v_out):
    def low(k):
        us = us_ref[k]
        return dot(jnp.concatenate([us, us], axis=1), vs_ref[k])

    low_ref[...] = low(0)
    diff = obs_ref[...] - low(1)
    sparse_ref[...] = diff - jnp.clip(diff, -SHRINK, SHRINK)
    u_out[...] = u_ref[...]
    v_out[...] = v_ref[...]


def slabs(observed, ust, vst, u, v):
    block = 512
    wide = pl.BlockSpec((block, NT_LOC), lambda i: (i, 0))
    u_spec = pl.BlockSpec((RANK, CH), lambda i: (0, 0))
    v_spec = pl.BlockSpec((64, RANK), lambda i: (0, 0))
    slab = jax.ShapeDtypeStruct((NS_LOC, NT_LOC), F32)
    return pl.pallas_call(
        slabs_kernel,
        grid=(NS_LOC // block,),
        out_shape=(slab, slab, jax.ShapeDtypeStruct((RANK, CH), F32), jax.ShapeDtypeStruct((64, RANK), F32)),
        in_specs=[
            wide,
            pl.BlockSpec((2, block, 128), lambda i: (0, i, 0)),
            pl.BlockSpec((2, 256, NT_LOC), lambda i: (0, 0, 0)),
            u_spec,
            v_spec,
        ],
        out_specs=(wide, wide, u_spec, v_spec),
        compiler_params=pltpu.CompilerParams(vmem_limit_bytes=SLABS_VMEM * 1024 * 1024),
        name="final_slabs",
    )(observed, ust, vst, u, v)


def shards(observed, u_start, v_start):
    ust, vst, ut, v_own = factors(observed, u_start.T, v_start)
    low, sparse, ut, v_own = slabs(observed, ust, vst, ut, v_own)
    return (low, sparse, ut.T, v_own)


def solution(mesh):
    return jax.shard_map(
        shards,
        mesh=mesh,
        in_specs=(P("rows", "cols"), P(("rows", "cols"), None), P(("cols", "rows"), None)),
        out_specs=(
            P("rows", "cols"),
            P("rows", "cols"),
            P(("rows", "cols"), None),
            P(("cols", "rows"), None),
        ),
        check_vma=False,
    )
```

```python
import functools

import jax
import jax.numpy as jnp
from jax import lax
from jax.experimental import pallas as pl
from jax.experimental.pallas import tpu as pltpu
from jax.sharding import PartitionSpec as P

ITERS = 4
SHRINK = 0.5
RIDGE = 1.0
RANK = 64
NY = 4
NR = 8
CH = 256
HALF = CH // 2
SUB = HALF // 2
NT_LOC = 512
NS_LOC = 4096
FACTOR_VMEM = 48
SLABS_VMEM = 16
MESH = pl.DeviceIdType.MESH
HI = lax.Precision.HIGHEST
F32 = jnp.float32
BF16 = jnp.bfloat16


def dot(a, b, dims=((1,), (0,)), precision=None):
    return lax.dot_general(a, b, (dims, ((), ())), precision=precision, preferred_element_type=F32)


def lanes(shape):
    return lax.broadcasted_iota(jnp.int32, shape, len(shape) - 1)


def sublanes(shape):
    return lax.broadcasted_iota(jnp.int32, shape, len(shape) - 2)


def roll64(m):
    return pltpu.roll(m, 64, 1)


def pack_gram(m):
    s = m + roll64(m)
    t = s[:64] + s[64:]
    return jnp.where(lanes((32, 128)) < 64, t[:32], t[32:])


def unpack_gram(k):
    kr = roll64(k)
    left = lanes((32, 128)) < 64
    return jnp.concatenate([jnp.where(left, k, kr), jnp.where(left, kr, k)], axis=0)


def twin_eye():
    return jnp.where((lanes((64, 128)) % 64) == sublanes((64, 128)), 1.0, 0.0).astype(F32)


def ridge_start(gg):
    eye = twin_eye()
    return jnp.where(lanes((64, 128)) < 64, gg + RIDGE * eye, eye)


def ridge_steps(m, first, last):
    rows = sublanes((64, 128))
    for k in range(first, last, 4):
        c = [jnp.broadcast_to(m[:, k + j : k + j + 1], (64, 128)) for j in range(4)]
        r = [m[k + i : k + i + 1, :] for i in range(4)]
        a = [[c[j][k + i : k + i + 1, :] for j in range(4)] for i in range(4)]

        def two(a00, a01, a10, a11):
            scale = 1.0 / (a00 * a11 - a01 * a10)
            return lambda x, y: ((a11 * x - a01 * y) * scale, (a00 * y - a10 * x) * scale)

        top = two(a[0][0], a[0][1], a[1][0], a[1][1])
        n0, n1 = top(r[0], r[1])
        t = [top(a[0][j], a[1][j]) for j in (2, 3)]
        low = [r[i] - a[i][0] * n0 - a[i][1] * n1 for i in (2, 3)]
        b = [[a[i][j] - a[i][0] * t[j - 2][0] - a[i][1] * t[j - 2][1] for j in (2, 3)] for i in (2, 3)]
        n2, n3 = two(b[0][0], b[0][1], b[1][0], b[1][1])(low[0], low[1])
        n0 = n0 - t[0][0] * n2 - t[1][0] * n3
        n1 = n1 - t[0][1] * n2 - t[1][1] * n3
        new = m - (c[0] * n0 + c[1] * n1) - (c[2] * n2 + c[3] * n3)
        for i, n in enumerate((n0, n1, n2, n3)):
            new = jnp.where(rows == k + i, n, new)
        m = new
    return m


def ridge_end(m):
    return jnp.where(lanes((64, 128)) < 64, roll64(m), m)


def ridge_inverse(gg):
    return ridge_end(ridge_steps(ridge_start(gg), 0, RANK))


def split(x):
    hi = x.astype(BF16)
    return hi, (x - hi.astype(F32)).astype(BF16)


def split3(x):
    hi, lo = split(x)
    rest = x - hi.astype(F32) - lo.astype(F32)
    return hi, lo, rest.astype(BF16)


def factor_kernel(
    obs_hbm, u0_hbm, v0_hbm,
    ust, vst, u_out, v_out,
    obs, rh, rl, part, r1, r2, pan, gw, gi, qt2, gu, wl, wr, qs, rq, rg, qp, vn,
    gv1, gv2, gva, gvb, gvc, gua, guc, u0_ref, v0_ref,
    obs_sem, u0_sem, v0_sem, s1s, s1r, s2s, s2r, ays, ayr, acs, acr,
    g1s, g1r, g2s, g2r, g3s, g3r, g4s, g4r, qs_s, qs_r, rg_s, rg_r, qa_s, qa_r, v0s, v0r,
):
    row = lax.axis_index("rows")
    col = lax.axis_index("cols")
    y, zh, co = col // 4, (col // 2) % 2, col % 2

    def cid(yy, zz, cc):
        return yy * 4 + zz * 2 + cc

    def pos(cc, yy, zz):
        return cc * 8 + yy * 2 + zz

    def to_chip(k):
        return (y + 1 + k // 2) % NY, (zh + 1 + k) % 2

    sib = {"cols": cid(y, zh, 1 - co)}

    def chip(k):
        yy, zz = to_chip(k)
        return {"cols": cid(yy, zz, co)}

    def rpeer(d):
        return {"rows": lax.rem(row + d, NR)}

    def rcopy(src, dst, ssem, rsem, dev):
        return pltpu.make_async_remote_copy(
            src_ref=src, dst_ref=dst, send_sem=ssem, recv_sem=rsem, device_id=dev, device_id_type=MESH
        )

    load_u = pltpu.make_async_copy(u0_hbm, u0_ref, u0_sem)
    load_u.start()
    load_v = pltpu.make_async_copy(v0_hbm, v0_ref, v0_sem)
    load_v.start()
    load = pltpu.make_async_copy(obs_hbm, obs, obs_sem)
    load.start()

    barrier = pltpu.get_barrier_semaphore()
    peers = [sib] + [chip(k) for k in range(7)] + [rpeer(d) for d in range(1, NR)]
    for dev in peers:
        pl.semaphore_signal(barrier, inc=1, device_id=dev, device_id_type=MESH)
    pl.semaphore_wait(barrier, len(peers))

    own = pos(co, y, zh)

    def slab_list(cc, h):
        first = [cid(n // 2, n % 2, cc) * CH + h * SUB for n in range(8)]
        return [pl.ds(pl.multiple_of(f + o, SUB), SUB) for o in (0, HALF) for f in first]

    def rows_of(ref, slabs, *lead):
        return jnp.concatenate([ref[(*lead, q, slice(None))] for q in slabs], axis=0)

    def put_rows(ref, slabs, value, *lead):
        for n, q in enumerate(slabs):
            ref[(*lead, q, slice(None))] = value[n * SUB : (n + 1) * SUB]

    my_half = pl.ds(pl.multiple_of(co * 16, 16), 16)

    def eight(cc):
        return pl.ds(pl.multiple_of(cc * 8, 8), 8)

    def set_apply(inv2):
        zero = jnp.zeros_like(inv2)
        g = jnp.concatenate(
            [jnp.concatenate([inv2, zero], axis=1), jnp.concatenate([zero, inv2], axis=1)], axis=0
        )
        g1, g2, g3 = split3(g)
        gw[0] = jnp.concatenate([g1, g1], axis=0)
        gw[1] = jnp.concatenate([g2, g2], axis=0)
        gw[2] = jnp.concatenate([g3, g1], axis=0)

    def solved(packed):
        p1, p2, p3 = split3(packed)
        p12 = jnp.concatenate([p1, p2], axis=1)
        p13 = jnp.concatenate([p1, p3], axis=1)
        return dot(p12, gw[0]) + (dot(p12, gw[1]) + dot(p13, gw[2]))

    def apply_chunks(cc, h, buf):
        u2 = solved(pan[h, eight(cc)].reshape(8 * SUB, 128))
        hi, lo = split(u2)
        left = (lanes(u2.shape) % 128) < 64
        st = jnp.where(left, hi.astype(F32), lo.astype(F32))
        us = jnp.concatenate([st[:, :128], st[:, 128:]], axis=0).astype(BF16)
        slabs = slab_list(cc, h)
        put_rows(ust, slabs, us, buf)
        return us, slabs

    def time_chunks(cc, h, buf):
        us, slabs = apply_chunks(cc, h, buf)
        ut = us.T
        gu[...] += dot(ut, us)
        right = jnp.concatenate([rows_of(rh, slabs), rows_of(rl, slabs)], axis=0)
        qt2[...] += dot(jnp.concatenate([ut, ut], axis=1), right)

    def wait_recv(dst, rsem):
        rcopy(dst, dst, rsem, rsem, sib).wait_recv()

    def wait_send(src, ssem):
        rcopy(src, src, ssem, ssem, sib).wait_send()

    def gather_start(h):
        mine = pan.at[h, own]
        for k in range(7):
            rcopy(mine, mine, ays.at[h], ayr.at[h, k], chip(k)).start()

    def gather_finish(process, buf):
        def pair(g, cc):
            return pos(cc, (y + NY - g) % NY, 0)

        def half(h, carry):
            wait_recv(pan.at[h, pos(co, y, 1 - zh)], ayr.at[h, 6])
            block = pan.at[h, pl.ds(pair(0, co), 2)]
            rcopy(block, block, acs.at[h], acr.at[h, 0], sib).start()
            for g in range(1, NY):
                for e in range(2):
                    wait_recv(pan.at[h, pair(g, co) + e], ayr.at[h, 2 * (g - 1) + (zh + 1 + e) % 2])
                block = pan.at[h, pl.ds(pair(g, co), 2)]
                rcopy(block, block, acs.at[h], acr.at[h, g], sib).start()
            process(co, h, buf)
            for g in range(NY):
                wait_recv(pan.at[h, pl.ds(pair(g, 1 - co), 2)], acr.at[h, g])
            process(1 - co, h, buf)
            return carry

        lax.fori_loop(0, 2, half, 0)

    def drain_cols():
        for h in range(2):
            wait_send(pan.at[h, pl.ds(0, 7)], ays.at[h])
            wait_send(pan.at[h, pl.ds(0, 8)], acs.at[h])

    def time_factor():
        return dot(gi[:, :RANK], qp[...].reshape(RANK, NT_LOC), precision=HI)

    def series_chunks(cc, h, buf):
        slabs = slab_list(cc, h)
        n = 8 * SUB
        us = rows_of(ust, slabs, buf)
        low = dot(jnp.concatenate([us, us], axis=1), vst[buf, :, :])
        remain = low + jnp.clip(rows_of(obs, slabs) - low, -SHRINK, SHRINK)
        hi, lo = split(remain)
        put_rows(rh, slabs, hi)
        put_rows(rl, slabs, lo)
        a = dot(jnp.concatenate([hi[:n], lo[:n]], axis=0), wl[...])
        b = dot(jnp.concatenate([hi[n:], lo[n:]], axis=0), wr[...])
        s = a + b
        s = s[:, :128] + s[:, 128:]
        part[h, eight(cc)] = (s[:n] + s[n:]).reshape(8, SUB, 128)

    load_v.wait()
    vn[row] = jnp.zeros((64, 128), F32)
    vn[row, :, pl.ds(0, RANK)] = v0_ref[...]
    for d in range(1, NR):
        rcopy(vn.at[row], vn.at[row], v0s, v0r, rpeer(d)).start()
    load_u.wait()
    u0 = jnp.concatenate([u0_ref[:, :HALF], u0_ref[:, HALF:]], axis=0).T
    for h in range(2):
        pan[h, own] = u0[h * SUB : (h + 1) * SUB]
        gather_start(h)
    set_apply(twin_eye())
    gather_finish(apply_chunks, 0)
    drain_cols()
    wait_recv(vn.at[pl.ds(0, NR - 1)], v0r)
    wait_send(vn.at[pl.ds(0, NR - 1)], v0s)
    qp[...] = vn[...].reshape(NT_LOC, 128).T[:RANK].reshape(NR, 8, NT_LOC)
    gi[...] = twin_eye()
    load.wait()

    def iteration(t, carry):
        buf = lax.rem(t, 2)
        nxt = 1 - buf
        vh, vl = split(time_factor())
        pair = jnp.concatenate([vh, vl], axis=0)
        gva[...] = pack_gram(dot(pair, pair, dims=((1,), (1,))))
        rcopy(gva, gv1, g1s, g1r, sib).start()
        vst[buf, :, :] = jnp.concatenate([vh, vh, vl, vl], axis=0)
        x = pair.astype(F32).T
        xr = roll64(x)
        left = lanes((NT_LOC, 128)) < 64
        zero = jnp.zeros_like(x)
        wl[...] = jnp.concatenate([jnp.where(left, x, zero), jnp.where(left, xr, zero)], axis=1).astype(BF16)
        wr[...] = jnp.concatenate([jnp.where(left, zero, xr), jnp.where(left, zero, x)], axis=1).astype(BF16)

        def sums(h, carry):
            series_chunks(1 - co, h, buf)
            rcopy(part.at[h, eight(1 - co)], r1.at[h], s1s.at[h], s1r.at[h], sib).start()

            @pl.when(h == 0)
            def _():
                rcopy(gva, gv1, g1s, g1r, sib).wait()
                gvb[...] = gva[...] + gv1[...]
                for k in range(7):
                    rcopy(gvb.at[my_half], gv2.at[k], g2s, g2r, chip(k)).start()

            series_chunks(co, h, buf)
            wait_recv(r1.at[h], s1r.at[h])
            part[h, eight(co)] += r1[h]
            for k in range(7):
                yy, zz = to_chip(k)
                rcopy(part.at[h, pos(co, yy, zz)], r2.at[h, k], s2s.at[h], s2r.at[h], chip(k)).start()
            return carry

        lax.fori_loop(0, 2, sums, 0)

        def total(h):
            wait_recv(r2.at[h], s2r.at[h])
            pan[h, own] = part[h, own] + jnp.sum(r2[h], axis=0)
            gather_start(h)

        gu[...] = jnp.zeros_like(gu)
        qt2[...] = jnp.zeros_like(qt2)
        wait_recv(gv2, g2r)
        gvc[my_half] = gvb[my_half] + jnp.sum(gv2[...], axis=0)
        swap = rcopy(gvc.at[my_half], gvc.at[my_half], g3s, g3r, sib)
        swap.start()
        total(0)
        swap.wait()
        set_apply(ridge_inverse(unpack_gram(gvc[...])))
        total(1)
        gather_finish(time_chunks, nxt)

        gua[...] = pack_gram(gu[...])
        for d in range(1, NR):
            rcopy(gua.at[my_half], rg.at[d - 1], rg_s, rg_r, rpeer(d)).start()
        q = qt2[...]
        qs[...] = (q[:64] + q[64:]).reshape(NR, 8, NT_LOC)
        for d in range(1, NR):
            peer = lax.rem(row + d, NR)
            rcopy(qs.at[peer], rq.at[d - 1], qs_s, qs_r, rpeer(d)).start()
        drain_cols()
        wait_send(gv2, g2s)
        for h in range(2):
            wait_send(r1.at[h], s1s.at[h])
            wait_send(r2.at[h], s2s.at[h])
        wait_recv(rg, rg_r)
        guc[my_half] = gua[my_half] + jnp.sum(rg[...], axis=0)
        swap = rcopy(guc.at[my_half], guc.at[my_half], g4s, g4r, sib)
        swap.start()
        wait_recv(rq, qs_r)
        qp[row] = qs[row] + jnp.sum(rq[...], axis=0)
        for d in range(1, NR):
            rcopy(qp.at[row], qp.at[row], qa_s, qa_r, rpeer(d)).start()
        swap.wait()
        gi[...] = ridge_inverse(unpack_gram(guc[...]))
        wait_send(rg, rg_s)
        wait_send(rq, qs_s)
        wait_recv(qp.at[pl.ds(0, NR - 1)], qa_r)
        wait_send(qp.at[pl.ds(0, NR - 1)], qa_s)
        return carry

    lax.fori_loop(0, ITERS, iteration, 0)

    u2 = solved(jnp.concatenate([pan[0, own], pan[1, own]], axis=0))
    u_out[:, pl.ds(0, HALF)] = u2[:, :128].T[:RANK]
    u_out[:, pl.ds(HALF, HALF)] = u2[:, 128:].T[:RANK]
    vt = time_factor()
    vh, vl = split(vt)
    vst[ITERS % 2, :, :] = jnp.concatenate([vh, vh, vl, vl], axis=0)
    vn[...] = jnp.concatenate([vt, vt], axis=0).T.reshape(NR, 64, 128)
    v_out[...] = vn[row, :, pl.ds(0, RANK)]


def factors(observed, ut, v):
    vm = pl.BlockSpec(memory_space=pltpu.VMEM)
    dma = pltpu.SemaphoreType.DMA
    return pl.pallas_call(
        factor_kernel,
        out_shape=(
            jax.ShapeDtypeStruct((2, NS_LOC, 128), BF16),
            jax.ShapeDtypeStruct((2, 256, NT_LOC), BF16),
            jax.ShapeDtypeStruct((RANK, CH), F32),
            jax.ShapeDtypeStruct((64, RANK), F32),
        ),
        in_specs=[pl.BlockSpec(memory_space=pl.ANY)] * 3,
        out_specs=(vm, vm, vm, vm),
        scratch_shapes=[
            pltpu.VMEM((NS_LOC, NT_LOC), F32),
            pltpu.VMEM((NS_LOC, NT_LOC), BF16),
            pltpu.VMEM((NS_LOC, NT_LOC), BF16),
            pltpu.VMEM((2, 16, SUB, 128), F32),
            pltpu.VMEM((2, 8, SUB, 128), F32),
            pltpu.VMEM((2, 7, SUB, 128), F32),
            pltpu.VMEM((2, 16, SUB, 128), F32),
            pltpu.VMEM((3, 256, 256), BF16),
            pltpu.VMEM((64, 128), F32),
            pltpu.VMEM((128, NT_LOC), F32),
            pltpu.VMEM((128, 128), F32),
            pltpu.VMEM((NT_LOC, 256), BF16),
            pltpu.VMEM((NT_LOC, 256), BF16),
            pltpu.VMEM((NR, 8, NT_LOC), F32),
            pltpu.VMEM((NR - 1, 8, NT_LOC), F32),
            pltpu.VMEM((NR - 1, 16, 128), F32),
            pltpu.VMEM((NR, 8, NT_LOC), F32),
            pltpu.VMEM((NR, 64, 128), F32),
            pltpu.VMEM((32, 128), F32),
            pltpu.VMEM((7, 16, 128), F32),
            pltpu.VMEM((32, 128), F32),
            pltpu.VMEM((32, 128), F32),
            pltpu.VMEM((32, 128), F32),
            pltpu.VMEM((32, 128), F32),
            pltpu.VMEM((32, 128), F32),
            pltpu.VMEM((RANK, CH), F32),
            pltpu.VMEM((64, RANK), F32),
            dma, dma, dma,
            dma((2,)), dma((2,)), dma((2,)), dma((2,)), dma((2,)), dma((2, 7)), dma((2,)), dma((2, 4)),
            dma, dma, dma, dma, dma, dma, dma, dma,
            dma, dma, dma, dma, dma, dma, dma, dma,
        ],
        compiler_params=pltpu.CompilerParams(
            collective_id=0, has_side_effects=True, vmem_limit_bytes=FACTOR_VMEM * 1024 * 1024
        ),
        cost_estimate=pl.CostEstimate(flops=13_000_000_000, bytes_accessed=12_000_000, transcendentals=0),
        name="factor_updates",
    )(observed, ut, v)


def slabs_kernel(obs_ref, us_ref, vs_ref, u_ref, v_ref, low_ref, sparse_ref, u_out, v_out):
    def low(k):
        us = us_ref[k]
        return dot(jnp.concatenate([us, us], axis=1), vs_ref[k])

    low_ref[...] = low(0)
    diff = obs_ref[...] - low(1)
    sparse_ref[...] = diff - jnp.clip(diff, -SHRINK, SHRINK)
    u_out[...] = u_ref[...]
    v_out[...] = v_ref[...]


def slabs(observed, ust, vst, u, v):
    block = 512
    wide = pl.BlockSpec((block, NT_LOC), lambda i: (i, 0))
    u_spec = pl.BlockSpec((RANK, CH), lambda i: (0, 0))
    v_spec = pl.BlockSpec((64, RANK), lambda i: (0, 0))
    slab = jax.ShapeDtypeStruct((NS_LOC, NT_LOC), F32)
    return pl.pallas_call(
        slabs_kernel,
        grid=(NS_LOC // block,),
        out_shape=(slab, slab, jax.ShapeDtypeStruct((RANK, CH), F32), jax.ShapeDtypeStruct((64, RANK), F32)),
        in_specs=[
            wide,
            pl.BlockSpec((2, block, 128), lambda i: (0, i, 0)),
            pl.BlockSpec((2, 256, NT_LOC), lambda i: (0, 0, 0)),
            u_spec,
            v_spec,
        ],
        out_specs=(wide, wide, u_spec, v_spec),
        compiler_params=pltpu.CompilerParams(vmem_limit_bytes=SLABS_VMEM * 1024 * 1024),
        name="final_slabs",
    )(observed, ust, vst, u, v)


def shards(observed, u_start, v_start):
    ust, vst, ut, v_own = factors(observed, u_start.T, v_start)
    low, sparse, ut, v_own = slabs(observed, ust, vst, ut, v_own)
    return (low, sparse, ut.T, v_own)


def solution(mesh):
    return jax.shard_map(
        shards,
        mesh=mesh,
        in_specs=(P("rows", "cols"), P(("rows", "cols"), None), P(("cols", "rows"), None)),
        out_specs=(
            P("rows", "cols"),
            P("rows", "cols"),
            P(("rows", "cols"), None),
            P(("cols", "rows"), None),
        ),
        check_vma=False,
    )
```

```python
import functools

import jax
import jax.numpy as jnp
from jax import lax
from jax.experimental import pallas as pl
from jax.experimental.pallas import tpu as pltpu
from jax.sharding import PartitionSpec as P

ITERS = 4
SHRINK = 0.5
RIDGE = 1.0
RANK = 64
NY = 4
NR = 8
CH = 256
HALF = CH // 2
SUB = HALF // 2
NT_LOC = 512
NS_LOC = 4096
FACTOR_VMEM = 48
SLABS_VMEM = 16
MESH = pl.DeviceIdType.MESH
HI = lax.Precision.HIGHEST
F32 = jnp.float32
BF16 = jnp.bfloat16


def dot(a, b, dims=((1,), (0,)), precision=None):
    return lax.dot_general(a, b, (dims, ((), ())), precision=precision, preferred_element_type=F32)


def lanes(shape):
    return lax.broadcasted_iota(jnp.int32, shape, len(shape) - 1)


def sublanes(shape):
    return lax.broadcasted_iota(jnp.int32, shape, len(shape) - 2)


def roll64(m):
    return pltpu.roll(m, 64, 1)


def pack_gram(m):
    s = m + roll64(m)
    t = s[:64] + s[64:]
    return jnp.where(lanes((32, 128)) < 64, t[:32], t[32:])


def unpack_gram(k):
    kr = roll64(k)
    left = lanes((32, 128)) < 64
    return jnp.concatenate([jnp.where(left, k, kr), jnp.where(left, kr, k)], axis=0)


def twin_eye():
    return jnp.where((lanes((64, 128)) % 64) == sublanes((64, 128)), 1.0, 0.0).astype(F32)


def ridge_start(gg):
    eye = twin_eye()
    return jnp.where(lanes((64, 128)) < 64, gg + RIDGE * eye, eye)


def ridge_steps(m, first, last):
    rows = sublanes((64, 128))
    for k in range(first, last, 4):
        c = [jnp.broadcast_to(m[:, k + j : k + j + 1], (64, 128)) for j in range(4)]
        r = [m[k + i : k + i + 1, :] for i in range(4)]
        a = [[c[j][k + i : k + i + 1, :] for j in range(4)] for i in range(4)]

        def two(a00, a01, a10, a11):
            scale = 1.0 / (a00 * a11 - a01 * a10)
            return lambda x, y: ((a11 * x - a01 * y) * scale, (a00 * y - a10 * x) * scale)

        top = two(a[0][0], a[0][1], a[1][0], a[1][1])
        n0, n1 = top(r[0], r[1])
        t = [top(a[0][j], a[1][j]) for j in (2, 3)]
        low = [r[i] - a[i][0] * n0 - a[i][1] * n1 for i in (2, 3)]
        b = [[a[i][j] - a[i][0] * t[j - 2][0] - a[i][1] * t[j - 2][1] for j in (2, 3)] for i in (2, 3)]
        n2, n3 = two(b[0][0], b[0][1], b[1][0], b[1][1])(low[0], low[1])
        n0 = n0 - t[0][0] * n2 - t[1][0] * n3
        n1 = n1 - t[0][1] * n2 - t[1][1] * n3
        new = m - (c[0] * n0 + c[1] * n1) - (c[2] * n2 + c[3] * n3)
        for i, n in enumerate((n0, n1, n2, n3)):
            new = jnp.where(rows == k + i, n, new)
        m = new
    return m


def ridge_end(m):
    return jnp.where(lanes((64, 128)) < 64, roll64(m), m)


def ridge_inverse(gg):
    return ridge_end(ridge_steps(ridge_start(gg), 0, RANK))


def split(x):
    hi = x.astype(BF16)
    return hi, (x - hi.astype(F32)).astype(BF16)


def split3(x):
    hi, lo = split(x)
    rest = x - hi.astype(F32) - lo.astype(F32)
    return hi, lo, rest.astype(BF16)


def factor_kernel(
    obs_hbm, u0_hbm, v0_hbm,
    ust, vst, u_out, v_out,
    obs, rh, rl, part, r1, r2, pan, gw, gi, qt2, gu, wl, wr, qs, rq, rg, qp, vn,
    gv1, gv2, gva, gvb, gvc, gua, guc, u0_ref, v0_ref,
    obs_sem, u0_sem, v0_sem, s1s, s1r, s2s, s2r, ays, ayr, acs, acr,
    g1s, g1r, g2s, g2r, g3s, g3r, g4s, g4r, qs_s, qs_r, rg_s, rg_r, qa_s, qa_r, v0s, v0r,
):
    row = lax.axis_index("rows")
    col = lax.axis_index("cols")
    y, zh, co = col // 4, (col // 2) % 2, col % 2

    def cid(yy, zz, cc):
        return yy * 4 + zz * 2 + cc

    def pos(cc, yy, zz):
        return cc * 8 + yy * 2 + zz

    def to_chip(k):
        return (y + 1 + k // 2) % NY, (zh + 1 + k) % 2

    sib = {"cols": cid(y, zh, 1 - co)}

    def chip(k):
        yy, zz = to_chip(k)
        return {"cols": cid(yy, zz, co)}

    def rpeer(d):
        return {"rows": lax.rem(row + d, NR)}

    def rcopy(src, dst, ssem, rsem, dev):
        return pltpu.make_async_remote_copy(
            src_ref=src, dst_ref=dst, send_sem=ssem, recv_sem=rsem, device_id=dev, device_id_type=MESH
        )

    load_u = pltpu.make_async_copy(u0_hbm, u0_ref, u0_sem)
    load_u.start()
    load_v = pltpu.make_async_copy(v0_hbm, v0_ref, v0_sem)
    load_v.start()
    load = pltpu.make_async_copy(obs_hbm, obs, obs_sem)
    load.start()

    barrier = pltpu.get_barrier_semaphore()
    peers = [sib] + [chip(k) for k in range(7)] + [rpeer(d) for d in range(1, NR)]
    for dev in peers:
        pl.semaphore_signal(barrier, inc=1, device_id=dev, device_id_type=MESH)
    pl.semaphore_wait(barrier, len(peers))

    own = pos(co, y, zh)

    def slab_list(cc, h):
        first = [cid(n // 2, n % 2, cc) * CH + h * SUB for n in range(8)]
        return [pl.ds(pl.multiple_of(f + o, SUB), SUB) for o in (0, HALF) for f in first]

    def rows_of(ref, slabs, *lead):
        return jnp.concatenate([ref[(*lead, q, slice(None))] for q in slabs], axis=0)

    def put_rows(ref, slabs, value, *lead):
        for n, q in enumerate(slabs):
            ref[(*lead, q, slice(None))] = value[n * SUB : (n + 1) * SUB]

    my_half = pl.ds(pl.multiple_of(co * 16, 16), 16)

    def eight(cc):
        return pl.ds(pl.multiple_of(cc * 8, 8), 8)

    def set_apply(inv2):
        zero = jnp.zeros_like(inv2)
        g = jnp.concatenate(
            [jnp.concatenate([inv2, zero], axis=1), jnp.concatenate([zero, inv2], axis=1)], axis=0
        )
        g1, g2, g3 = split3(g)
        gw[0] = jnp.concatenate([g1, g1], axis=0)
        gw[1] = jnp.concatenate([g2, g2], axis=0)
        gw[2] = jnp.concatenate([g3, g1], axis=0)

    def solved(packed):
        p1, p2, p3 = split3(packed)
        p12 = jnp.concatenate([p1, p2], axis=1)
        p13 = jnp.concatenate([p1, p3], axis=1)
        return dot(p12, gw[0]) + (dot(p12, gw[1]) + dot(p13, gw[2]))

    def apply_chunks(cc, h, buf):
        u2 = solved(pan[h, eight(cc)].reshape(8 * SUB, 128))
        hi, lo = split(u2)
        left = (lanes(u2.shape) % 128) < 64
        st = jnp.where(left, hi.astype(F32), lo.astype(F32))
        us = jnp.concatenate([st[:, :128], st[:, 128:]], axis=0).astype(BF16)
        slabs = slab_list(cc, h)
        put_rows(ust, slabs, us, buf)
        return us, slabs

    def time_chunks(cc, h, buf):
        us, slabs = apply_chunks(cc, h, buf)
        ut = us.T
        gu[...] += dot(ut, us)
        right = jnp.concatenate([rows_of(rh, slabs), rows_of(rl, slabs)], axis=0)
        qt2[...] += dot(jnp.concatenate([ut, ut], axis=1), right)

    def wait_recv(dst, rsem):
        rcopy(dst, dst, rsem, rsem, sib).wait_recv()

    def wait_send(src, ssem):
        rcopy(src, src, ssem, ssem, sib).wait_send()

    def gather_start(h):
        mine = pan.at[h, own]
        for k in range(7):
            rcopy(mine, mine, ays.at[h], ayr.at[h, k], chip(k)).start()

    def gather_finish(process, buf):
        def pair(g, cc):
            return pos(cc, (y + NY - g) % NY, 0)

        def half(h, carry):
            wait_recv(pan.at[h, pos(co, y, 1 - zh)], ayr.at[h, 6])
            block = pan.at[h, pl.ds(pair(0, co), 2)]
            rcopy(block, block, acs.at[h], acr.at[h, 0], sib).start()
            for g in range(1, NY):
                for e in range(2):
                    wait_recv(pan.at[h, pair(g, co) + e], ayr.at[h, 2 * (g - 1) + (zh + 1 + e) % 2])
                block = pan.at[h, pl.ds(pair(g, co), 2)]
                rcopy(block, block, acs.at[h], acr.at[h, g], sib).start()
            process(co, h, buf)
            for g in range(NY):
                wait_recv(pan.at[h, pl.ds(pair(g, 1 - co), 2)], acr.at[h, g])
            process(1 - co, h, buf)
            return carry

        lax.fori_loop(0, 2, half, 0)

    def drain_cols():
        for h in range(2):
            wait_send(pan.at[h, pl.ds(0, 7)], ays.at[h])
            wait_send(pan.at[h, pl.ds(0, 8)], acs.at[h])

    def time_factor():
        return dot(gi[:, :RANK], qp[...].reshape(RANK, NT_LOC), precision=HI)

    def series_chunks(cc, h, buf):
        slabs = slab_list(cc, h)
        n = 8 * SUB
        us = rows_of(ust, slabs, buf)
        low = dot(jnp.concatenate([us, us], axis=1), vst[buf, :, :])
        remain = low + jnp.clip(rows_of(obs, slabs) - low, -SHRINK, SHRINK)
        hi, lo = split(remain)
        put_rows(rh, slabs, hi)
        put_rows(rl, slabs, lo)
        a = dot(jnp.concatenate([hi[:n], lo[:n]], axis=0), wl[...])
        b = dot(jnp.concatenate([hi[n:], lo[n:]], axis=0), wr[...])
        s = a + b
        s = s[:, :128] + s[:, 128:]
        part[h, eight(cc)] = (s[:n] + s[n:]).reshape(8, SUB, 128)

    load_v.wait()
    vn[row] = jnp.zeros((64, 128), F32)
    vn[row, :, pl.ds(0, RANK)] = v0_ref[...]
    for d in range(1, NR):
        rcopy(vn.at[row], vn.at[row], v0s, v0r, rpeer(d)).start()
    load_u.wait()
    u0 = jnp.concatenate([u0_ref[:, :HALF], u0_ref[:, HALF:]], axis=0).T
    for h in range(2):
        pan[h, own] = u0[h * SUB : (h + 1) * SUB]
        gather_start(h)
    set_apply(twin_eye())
    gather_finish(apply_chunks, 0)
    drain_cols()
    wait_recv(vn.at[pl.ds(0, NR - 1)], v0r)
    wait_send(vn.at[pl.ds(0, NR - 1)], v0s)
    qp[...] = vn[...].reshape(NT_LOC, 128).T[:RANK].reshape(NR, 8, NT_LOC)
    gi[...] = twin_eye()
    load.wait()

    def iteration(t, carry):
        buf = lax.rem(t, 2)
        nxt = 1 - buf
        vh, vl = split(time_factor())
        pair = jnp.concatenate([vh, vl], axis=0)
        gva[...] = pack_gram(dot(pair, pair, dims=((1,), (1,))))
        rcopy(gva, gv1, g1s, g1r, sib).start()
        vst[buf, :, :] = jnp.concatenate([vh, vh, vl, vl], axis=0)
        x = pair.astype(F32).T
        xr = roll64(x)
        left = lanes((NT_LOC, 128)) < 64
        zero = jnp.zeros_like(x)
        wl[...] = jnp.concatenate([jnp.where(left, x, zero), jnp.where(left, xr, zero)], axis=1).astype(BF16)
        wr[...] = jnp.concatenate([jnp.where(left, zero, xr), jnp.where(left, zero, x)], axis=1).astype(BF16)

        for h in range(2):
            series_chunks(1 - co, h, buf)
            rcopy(part.at[h, eight(1 - co)], r1.at[h], s1s.at[h], s1r.at[h], sib).start()

            if h == 0:
                rcopy(gva, gv1, g1s, g1r, sib).wait()
                gvb[...] = gva[...] + gv1[...]
                for k in range(7):
                    rcopy(gvb.at[my_half], gv2.at[k], g2s, g2r, chip(k)).start()

            series_chunks(co, h, buf)
            wait_recv(r1.at[h], s1r.at[h])
            part[h, eight(co)] += r1[h]
            for k in range(7):
                yy, zz = to_chip(k)
                rcopy(part.at[h, pos(co, yy, zz)], r2.at[h, k], s2s.at[h], s2r.at[h], chip(k)).start()

        def total(h):
            wait_recv(r2.at[h], s2r.at[h])
            pan[h, own] = part[h, own] + jnp.sum(r2[h], axis=0)
            gather_start(h)

        gu[...] = jnp.zeros_like(gu)
        qt2[...] = jnp.zeros_like(qt2)
        wait_recv(gv2, g2r)
        gvc[my_half] = gvb[my_half] + jnp.sum(gv2[...], axis=0)
        swap = rcopy(gvc.at[my_half], gvc.at[my_half], g3s, g3r, sib)
        swap.start()
        total(0)
        swap.wait()
        set_apply(ridge_inverse(unpack_gram(gvc[...])))
        total(1)
        gather_finish(time_chunks, nxt)

        gua[...] = pack_gram(gu[...])
        for d in range(1, NR):
            rcopy(gua.at[my_half], rg.at[d - 1], rg_s, rg_r, rpeer(d)).start()
        q = qt2[...]
        qs[...] = (q[:64] + q[64:]).reshape(NR, 8, NT_LOC)
        for d in range(1, NR):
            peer = lax.rem(row + d, NR)
            rcopy(qs.at[peer], rq.at[d - 1], qs_s, qs_r, rpeer(d)).start()
        drain_cols()
        wait_send(gv2, g2s)
        for h in range(2):
            wait_send(r1.at[h], s1s.at[h])
            wait_send(r2.at[h], s2s.at[h])
        wait_recv(rg, rg_r)
        guc[my_half] = gua[my_half] + jnp.sum(rg[...], axis=0)
        swap = rcopy(guc.at[my_half], guc.at[my_half], g4s, g4r, sib)
        swap.start()
        wait_recv(rq, qs_r)
        qp[row] = qs[row] + jnp.sum(rq[...], axis=0)
        for d in range(1, NR):
            rcopy(qp.at[row], qp.at[row], qa_s, qa_r, rpeer(d)).start()
        swap.wait()
        gi[...] = ridge_inverse(unpack_gram(guc[...]))
        wait_send(rg, rg_s)
        wait_send(rq, qs_s)
        wait_recv(qp.at[pl.ds(0, NR - 1)], qa_r)
        wait_send(qp.at[pl.ds(0, NR - 1)], qa_s)
        return carry

    lax.fori_loop(0, ITERS, iteration, 0)

    u2 = solved(jnp.concatenate([pan[0, own], pan[1, own]], axis=0))
    u_out[:, pl.ds(0, HALF)] = u2[:, :128].T[:RANK]
    u_out[:, pl.ds(HALF, HALF)] = u2[:, 128:].T[:RANK]
    vt = time_factor()
    vh, vl = split(vt)
    vst[ITERS % 2, :, :] = jnp.concatenate([vh, vh, vl, vl], axis=0)
    vn[...] = jnp.concatenate([vt, vt], axis=0).T.reshape(NR, 64, 128)
    v_out[...] = vn[row, :, pl.ds(0, RANK)]


def factors(observed, ut, v):
    vm = pl.BlockSpec(memory_space=pltpu.VMEM)
    dma = pltpu.SemaphoreType.DMA
    return pl.pallas_call(
        factor_kernel,
        out_shape=(
            jax.ShapeDtypeStruct((2, NS_LOC, 128), BF16),
            jax.ShapeDtypeStruct((2, 256, NT_LOC), BF16),
            jax.ShapeDtypeStruct((RANK, CH), F32),
            jax.ShapeDtypeStruct((64, RANK), F32),
        ),
        in_specs=[pl.BlockSpec(memory_space=pl.ANY)] * 3,
        out_specs=(vm, vm, vm, vm),
        scratch_shapes=[
            pltpu.VMEM((NS_LOC, NT_LOC), F32),
            pltpu.VMEM((NS_LOC, NT_LOC), BF16),
            pltpu.VMEM((NS_LOC, NT_LOC), BF16),
            pltpu.VMEM((2, 16, SUB, 128), F32),
            pltpu.VMEM((2, 8, SUB, 128), F32),
            pltpu.VMEM((2, 7, SUB, 128), F32),
            pltpu.VMEM((2, 16, SUB, 128), F32),
            pltpu.VMEM((3, 256, 256), BF16),
            pltpu.VMEM((64, 128), F32),
            pltpu.VMEM((128, NT_LOC), F32),
            pltpu.VMEM((128, 128), F32),
            pltpu.VMEM((NT_LOC, 256), BF16),
            pltpu.VMEM((NT_LOC, 256), BF16),
            pltpu.VMEM((NR, 8, NT_LOC), F32),
            pltpu.VMEM((NR - 1, 8, NT_LOC), F32),
            pltpu.VMEM((NR - 1, 16, 128), F32),
            pltpu.VMEM((NR, 8, NT_LOC), F32),
            pltpu.VMEM((NR, 64, 128), F32),
            pltpu.VMEM((32, 128), F32),
            pltpu.VMEM((7, 16, 128), F32),
            pltpu.VMEM((32, 128), F32),
            pltpu.VMEM((32, 128), F32),
            pltpu.VMEM((32, 128), F32),
            pltpu.VMEM((32, 128), F32),
            pltpu.VMEM((32, 128), F32),
            pltpu.VMEM((RANK, CH), F32),
            pltpu.VMEM((64, RANK), F32),
            dma, dma, dma,
            dma((2,)), dma((2,)), dma((2,)), dma((2,)), dma((2,)), dma((2, 7)), dma((2,)), dma((2, 4)),
            dma, dma, dma, dma, dma, dma, dma, dma,
            dma, dma, dma, dma, dma, dma, dma, dma,
        ],
        compiler_params=pltpu.CompilerParams(
            collective_id=0, has_side_effects=True, vmem_limit_bytes=FACTOR_VMEM * 1024 * 1024
        ),
        cost_estimate=pl.CostEstimate(flops=13_000_000_000, bytes_accessed=12_000_000, transcendentals=0),
        name="factor_updates",
    )(observed, ut, v)


def slabs_kernel(obs_ref, us_ref, vs_ref, u_ref, v_ref, low_ref, sparse_ref, u_out, v_out):
    def low(k):
        us = us_ref[k]
        return dot(jnp.concatenate([us, us], axis=1), vs_ref[k])

    low_ref[...] = low(0)
    diff = obs_ref[...] - low(1)
    sparse_ref[...] = diff - jnp.clip(diff, -SHRINK, SHRINK)
    u_out[...] = u_ref[...]
    v_out[...] = v_ref[...]


def slabs(observed, ust, vst, u, v):
    block = 512
    wide = pl.BlockSpec((block, NT_LOC), lambda i: (i, 0))
    u_spec = pl.BlockSpec((RANK, CH), lambda i: (0, 0))
    v_spec = pl.BlockSpec((64, RANK), lambda i: (0, 0))
    slab = jax.ShapeDtypeStruct((NS_LOC, NT_LOC), F32)
    return pl.pallas_call(
        slabs_kernel,
        grid=(NS_LOC // block,),
        out_shape=(slab, slab, jax.ShapeDtypeStruct((RANK, CH), F32), jax.ShapeDtypeStruct((64, RANK), F32)),
        in_specs=[
            wide,
            pl.BlockSpec((2, block, 128), lambda i: (0, i, 0)),
            pl.BlockSpec((2, 256, NT_LOC), lambda i: (0, 0, 0)),
            u_spec,
            v_spec,
        ],
        out_specs=(wide, wide, u_spec, v_spec),
        compiler_params=pltpu.CompilerParams(vmem_limit_bytes=SLABS_VMEM * 1024 * 1024),
        name="final_slabs",
    )(observed, ust, vst, u, v)


def shards(observed, u_start, v_start):
    ust, vst, ut, v_own = factors(observed, u_start.T, v_start)
    low, sparse, ut, v_own = slabs(observed, ust, vst, ut, v_own)
    return (low, sparse, ut.T, v_own)


def solution(mesh):
    return jax.shard_map(
        shards,
        mesh=mesh,
        in_specs=(P("rows", "cols"), P(("rows", "cols"), None), P(("cols", "rows"), None)),
        out_specs=(
            P("rows", "cols"),
            P("rows", "cols"),
            P(("rows", "cols"), None),
            P(("cols", "rows"), None),
        ),
        check_vma=False,
    )
```

```python
import functools

import jax
import jax.numpy as jnp
from jax import lax
from jax.experimental import pallas as pl
from jax.experimental.pallas import tpu as pltpu
from jax.sharding import PartitionSpec as P

ITERS = 4
SHRINK = 0.5
RIDGE = 1.0
RANK = 64
NY = 4
NR = 8
CH = 256
HALF = CH // 2
SUB = HALF // 2
NT_LOC = 512
NS_LOC = 4096
FACTOR_VMEM = 48
SLABS_VMEM = 16
MESH = pl.DeviceIdType.MESH
HI = lax.Precision.HIGHEST
F32 = jnp.float32
BF16 = jnp.bfloat16


def dot(a, b, dims=((1,), (0,)), precision=None):
    return lax.dot_general(a, b, (dims, ((), ())), precision=precision, preferred_element_type=F32)


def lanes(shape):
    return lax.broadcasted_iota(jnp.int32, shape, len(shape) - 1)


def sublanes(shape):
    return lax.broadcasted_iota(jnp.int32, shape, len(shape) - 2)


def roll64(m):
    return pltpu.roll(m, 64, 1)


def pack_gram(m):
    s = m + roll64(m)
    t = s[:64] + s[64:]
    return jnp.where(lanes((32, 128)) < 64, t[:32], t[32:])


def unpack_gram(k):
    kr = roll64(k)
    left = lanes((32, 128)) < 64
    return jnp.concatenate([jnp.where(left, k, kr), jnp.where(left, kr, k)], axis=0)


def twin_eye():
    return jnp.where((lanes((64, 128)) % 64) == sublanes((64, 128)), 1.0, 0.0).astype(F32)


def ridge_start(gg):
    eye = twin_eye()
    return jnp.where(lanes((64, 128)) < 64, gg + RIDGE * eye, eye)


def ridge_steps(m, first, last):
    rows = sublanes((64, 128))
    for k in range(first, last, 4):
        c = [jnp.broadcast_to(m[:, k + j : k + j + 1], (64, 128)) for j in range(4)]
        r = [m[k + i : k + i + 1, :] for i in range(4)]
        a = [[c[j][k + i : k + i + 1, :] for j in range(4)] for i in range(4)]

        def two(a00, a01, a10, a11):
            scale = 1.0 / (a00 * a11 - a01 * a10)
            return lambda x, y: ((a11 * x - a01 * y) * scale, (a00 * y - a10 * x) * scale)

        top = two(a[0][0], a[0][1], a[1][0], a[1][1])
        n0, n1 = top(r[0], r[1])
        t = [top(a[0][j], a[1][j]) for j in (2, 3)]
        low = [r[i] - a[i][0] * n0 - a[i][1] * n1 for i in (2, 3)]
        b = [[a[i][j] - a[i][0] * t[j - 2][0] - a[i][1] * t[j - 2][1] for j in (2, 3)] for i in (2, 3)]
        n2, n3 = two(b[0][0], b[0][1], b[1][0], b[1][1])(low[0], low[1])
        n0 = n0 - t[0][0] * n2 - t[1][0] * n3
        n1 = n1 - t[0][1] * n2 - t[1][1] * n3
        new = m - (c[0] * n0 + c[1] * n1) - (c[2] * n2 + c[3] * n3)
        for i, n in enumerate((n0, n1, n2, n3)):
            new = jnp.where(rows == k + i, n, new)
        m = new
    return m


def ridge_end(m):
    return jnp.where(lanes((64, 128)) < 64, roll64(m), m)


def ridge_inverse(gg):
    return ridge_end(ridge_steps(ridge_start(gg), 0, RANK))


def split(x):
    hi = x.astype(BF16)
    return hi, (x - hi.astype(F32)).astype(BF16)


def split3(x):
    hi, lo = split(x)
    rest = x - hi.astype(F32) - lo.astype(F32)
    return hi, lo, rest.astype(BF16)


def factor_kernel(
    obs_hbm, u0_hbm, v0_hbm,
    ust, vst, u_out, v_out,
    obs, rh, rl, part, r1, r2, pan, gw, gi, qt2, gu, wl, wr, qs, rq, rg, qp, vn,
    gv1, gv2, gva, gvb, gvc, gua, guc, u0_ref, v0_ref,
    obs_sem, u0_sem, v0_sem, s1s, s1r, s2s, s2r, ays, ayr, acs, acr,
    g1s, g1r, g2s, g2r, g3s, g3r, g4s, g4r, qs_s, qs_r, rg_s, rg_r, qa_s, qa_r, v0s, v0r,
):
    row = lax.axis_index("rows")
    col = lax.axis_index("cols")
    y, zh, co = col // 4, (col // 2) % 2, col % 2

    def cid(yy, zz, cc):
        return yy * 4 + zz * 2 + cc

    def pos(cc, yy, zz):
        return cc * 8 + yy * 2 + zz

    def to_chip(k):
        return (y + 1 + k // 2) % NY, (zh + 1 + k) % 2

    sib = {"cols": cid(y, zh, 1 - co)}

    def chip(k):
        yy, zz = to_chip(k)
        return {"cols": cid(yy, zz, co)}

    def rpeer(d):
        return {"rows": lax.rem(row + d, NR)}

    def rcopy(src, dst, ssem, rsem, dev):
        return pltpu.make_async_remote_copy(
            src_ref=src, dst_ref=dst, send_sem=ssem, recv_sem=rsem, device_id=dev, device_id_type=MESH
        )

    load_u = pltpu.make_async_copy(u0_hbm, u0_ref, u0_sem)
    load_u.start()
    load_v = pltpu.make_async_copy(v0_hbm, v0_ref, v0_sem)
    load_v.start()
    load = pltpu.make_async_copy(obs_hbm, obs, obs_sem)
    load.start()

    barrier = pltpu.get_barrier_semaphore()
    peers = [sib] + [chip(k) for k in range(7)] + [rpeer(d) for d in range(1, NR)]
    for dev in peers:
        pl.semaphore_signal(barrier, inc=1, device_id=dev, device_id_type=MESH)
    pl.semaphore_wait(barrier, len(peers))

    own = pos(co, y, zh)

    def slab_list(cc, h):
        first = [cid(n // 2, n % 2, cc) * CH + h * SUB for n in range(8)]
        return [pl.ds(pl.multiple_of(f + o, SUB), SUB) for o in (0, HALF) for f in first]

    def rows_of(ref, slabs, *lead):
        return jnp.concatenate([ref[(*lead, q, slice(None))] for q in slabs], axis=0)

    def put_rows(ref, slabs, value, *lead):
        for n, q in enumerate(slabs):
            ref[(*lead, q, slice(None))] = value[n * SUB : (n + 1) * SUB]

    my_half = pl.ds(pl.multiple_of(co * 16, 16), 16)

    def eight(cc):
        return pl.ds(pl.multiple_of(cc * 8, 8), 8)

    def set_apply(inv2):
        zero = jnp.zeros_like(inv2)
        g = jnp.concatenate(
            [jnp.concatenate([inv2, zero], axis=1), jnp.concatenate([zero, inv2], axis=1)], axis=0
        )
        g1, g2, g3 = split3(g)
        gw[0] = jnp.concatenate([g1, g1], axis=0)
        gw[1] = jnp.concatenate([g2, g2], axis=0)
        gw[2] = jnp.concatenate([g3, g1], axis=0)

    def solved(packed):
        p1, p2, p3 = split3(packed)
        p12 = jnp.concatenate([p1, p2], axis=1)
        p13 = jnp.concatenate([p1, p3], axis=1)
        return dot(p12, gw[0]) + (dot(p12, gw[1]) + dot(p13, gw[2]))

    def apply_chunks(cc, h, buf):
        u2 = solved(pan[h, eight(cc)].reshape(8 * SUB, 128))
        hi, lo = split(u2)
        left = (lanes(u2.shape) % 128) < 64
        st = jnp.where(left, hi.astype(F32), lo.astype(F32))
        us = jnp.concatenate([st[:, :128], st[:, 128:]], axis=0).astype(BF16)
        slabs = slab_list(cc, h)
        put_rows(ust, slabs, us, buf)
        return us, slabs

    def time_chunks(cc, h, buf):
        us, slabs = apply_chunks(cc, h, buf)
        ut = us.T
        gu[...] += dot(ut, us)
        right = jnp.concatenate([rows_of(rh, slabs), rows_of(rl, slabs)], axis=0)
        qt2[...] += dot(jnp.concatenate([ut, ut], axis=1), right)

    def wait_recv(dst, rsem):
        rcopy(dst, dst, rsem, rsem, sib).wait_recv()

    def wait_send(src, ssem):
        rcopy(src, src, ssem, ssem, sib).wait_send()

    def gather_start(h):
        mine = pan.at[h, own]
        for k in range(7):
            rcopy(mine, mine, ays.at[h], ayr.at[h, k], chip(k)).start()

    def gather_finish(process, buf):
        def pair(g, cc):
            return pos(cc, (y + NY - g) % NY, 0)

        def half(h, carry):
            wait_recv(pan.at[h, pos(co, y, 1 - zh)], ayr.at[h, 6])
            block = pan.at[h, pl.ds(pair(0, co), 2)]
            rcopy(block, block, acs.at[h], acr.at[h, 0], sib).start()
            for g in range(1, NY):
                for e in range(2):
                    wait_recv(pan.at[h, pair(g, co) + e], ayr.at[h, 2 * (g - 1) + (zh + 1 + e) % 2])
                block = pan.at[h, pl.ds(pair(g, co), 2)]
                rcopy(block, block, acs.at[h], acr.at[h, g], sib).start()
            process(co, h, buf)
            for g in range(NY):
                wait_recv(pan.at[h, pl.ds(pair(g, 1 - co), 2)], acr.at[h, g])
            process(1 - co, h, buf)
            return carry

        for h in range(2):
            half(h, 0)

    def drain_cols():
        for h in range(2):
            wait_send(pan.at[h, pl.ds(0, 7)], ays.at[h])
            wait_send(pan.at[h, pl.ds(0, 8)], acs.at[h])

    def time_factor():
        return dot(gi[:, :RANK], qp[...].reshape(RANK, NT_LOC), precision=HI)

    def series_chunks(cc, h, buf):
        slabs = slab_list(cc, h)
        n = 8 * SUB
        us = rows_of(ust, slabs, buf)
        low = dot(jnp.concatenate([us, us], axis=1), vst[buf, :, :])
        remain = low + jnp.clip(rows_of(obs, slabs) - low, -SHRINK, SHRINK)
        hi, lo = split(remain)
        put_rows(rh, slabs, hi)
        put_rows(rl, slabs, lo)
        a = dot(jnp.concatenate([hi[:n], lo[:n]], axis=0), wl[...])
        b = dot(jnp.concatenate([hi[n:], lo[n:]], axis=0), wr[...])
        s = a + b
        s = s[:, :128] + s[:, 128:]
        part[h, eight(cc)] = (s[:n] + s[n:]).reshape(8, SUB, 128)

    load_v.wait()
    vn[row] = jnp.zeros((64, 128), F32)
    vn[row, :, pl.ds(0, RANK)] = v0_ref[...]
    for d in range(1, NR):
        rcopy(vn.at[row], vn.at[row], v0s, v0r, rpeer(d)).start()
    load_u.wait()
    u0 = jnp.concatenate([u0_ref[:, :HALF], u0_ref[:, HALF:]], axis=0).T
    for h in range(2):
        pan[h, own] = u0[h * SUB : (h + 1) * SUB]
        gather_start(h)
    set_apply(twin_eye())
    gather_finish(apply_chunks, 0)
    drain_cols()
    wait_recv(vn.at[pl.ds(0, NR - 1)], v0r)
    wait_send(vn.at[pl.ds(0, NR - 1)], v0s)
    qp[...] = vn[...].reshape(NT_LOC, 128).T[:RANK].reshape(NR, 8, NT_LOC)
    gi[...] = twin_eye()
    load.wait()

    def iteration(t, carry):
        buf = lax.rem(t, 2)
        nxt = 1 - buf
        vh, vl = split(time_factor())
        pair = jnp.concatenate([vh, vl], axis=0)
        gva[...] = pack_gram(dot(pair, pair, dims=((1,), (1,))))
        rcopy(gva, gv1, g1s, g1r, sib).start()
        vst[buf, :, :] = jnp.concatenate([vh, vh, vl, vl], axis=0)
        x = pair.astype(F32).T
        xr = roll64(x)
        left = lanes((NT_LOC, 128)) < 64
        zero = jnp.zeros_like(x)
        wl[...] = jnp.concatenate([jnp.where(left, x, zero), jnp.where(left, xr, zero)], axis=1).astype(BF16)
        wr[...] = jnp.concatenate([jnp.where(left, zero, xr), jnp.where(left, zero, x)], axis=1).astype(BF16)

        for h in range(2):
            series_chunks(1 - co, h, buf)
            rcopy(part.at[h, eight(1 - co)], r1.at[h], s1s.at[h], s1r.at[h], sib).start()

            if h == 0:
                rcopy(gva, gv1, g1s, g1r, sib).wait()
                gvb[...] = gva[...] + gv1[...]
                for k in range(7):
                    rcopy(gvb.at[my_half], gv2.at[k], g2s, g2r, chip(k)).start()

            series_chunks(co, h, buf)
            wait_recv(r1.at[h], s1r.at[h])
            part[h, eight(co)] += r1[h]
            for k in range(7):
                yy, zz = to_chip(k)
                rcopy(part.at[h, pos(co, yy, zz)], r2.at[h, k], s2s.at[h], s2r.at[h], chip(k)).start()

        def total(h):
            wait_recv(r2.at[h], s2r.at[h])
            pan[h, own] = part[h, own] + jnp.sum(r2[h], axis=0)
            gather_start(h)

        gu[...] = jnp.zeros_like(gu)
        qt2[...] = jnp.zeros_like(qt2)
        wait_recv(gv2, g2r)
        gvc[my_half] = gvb[my_half] + jnp.sum(gv2[...], axis=0)
        swap = rcopy(gvc.at[my_half], gvc.at[my_half], g3s, g3r, sib)
        swap.start()
        total(0)
        swap.wait()
        set_apply(ridge_inverse(unpack_gram(gvc[...])))
        total(1)
        gather_finish(time_chunks, nxt)

        gua[...] = pack_gram(gu[...])
        for d in range(1, NR):
            rcopy(gua.at[my_half], rg.at[d - 1], rg_s, rg_r, rpeer(d)).start()
        q = qt2[...]
        qs[...] = (q[:64] + q[64:]).reshape(NR, 8, NT_LOC)
        for d in range(1, NR):
            peer = lax.rem(row + d, NR)
            rcopy(qs.at[peer], rq.at[d - 1], qs_s, qs_r, rpeer(d)).start()
        drain_cols()
        wait_send(gv2, g2s)
        for h in range(2):
            wait_send(r1.at[h], s1s.at[h])
            wait_send(r2.at[h], s2s.at[h])
        wait_recv(rg, rg_r)
        guc[my_half] = gua[my_half] + jnp.sum(rg[...], axis=0)
        swap = rcopy(guc.at[my_half], guc.at[my_half], g4s, g4r, sib)
        swap.start()
        wait_recv(rq, qs_r)
        qp[row] = qs[row] + jnp.sum(rq[...], axis=0)
        for d in range(1, NR):
            rcopy(qp.at[row], qp.at[row], qa_s, qa_r, rpeer(d)).start()
        swap.wait()
        gi[...] = ridge_inverse(unpack_gram(guc[...]))
        wait_send(rg, rg_s)
        wait_send(rq, qs_s)
        wait_recv(qp.at[pl.ds(0, NR - 1)], qa_r)
        wait_send(qp.at[pl.ds(0, NR - 1)], qa_s)
        return carry

    lax.fori_loop(0, ITERS, iteration, 0)

    u2 = solved(jnp.concatenate([pan[0, own], pan[1, own]], axis=0))
    u_out[:, pl.ds(0, HALF)] = u2[:, :128].T[:RANK]
    u_out[:, pl.ds(HALF, HALF)] = u2[:, 128:].T[:RANK]
    vt = time_factor()
    vh, vl = split(vt)
    vst[ITERS % 2, :, :] = jnp.concatenate([vh, vh, vl, vl], axis=0)
    vn[...] = jnp.concatenate([vt, vt], axis=0).T.reshape(NR, 64, 128)
    v_out[...] = vn[row, :, pl.ds(0, RANK)]


def factors(observed, ut, v):
    vm = pl.BlockSpec(memory_space=pltpu.VMEM)
    dma = pltpu.SemaphoreType.DMA
    return pl.pallas_call(
        factor_kernel,
        out_shape=(
            jax.ShapeDtypeStruct((2, NS_LOC, 128), BF16),
            jax.ShapeDtypeStruct((2, 256, NT_LOC), BF16),
            jax.ShapeDtypeStruct((RANK, CH), F32),
            jax.ShapeDtypeStruct((64, RANK), F32),
        ),
        in_specs=[pl.BlockSpec(memory_space=pl.ANY)] * 3,
        out_specs=(vm, vm, vm, vm),
        scratch_shapes=[
            pltpu.VMEM((NS_LOC, NT_LOC), F32),
            pltpu.VMEM((NS_LOC, NT_LOC), BF16),
            pltpu.VMEM((NS_LOC, NT_LOC), BF16),
            pltpu.VMEM((2, 16, SUB, 128), F32),
            pltpu.VMEM((2, 8, SUB, 128), F32),
            pltpu.VMEM((2, 7, SUB, 128), F32),
            pltpu.VMEM((2, 16, SUB, 128), F32),
            pltpu.VMEM((3, 256, 256), BF16),
            pltpu.VMEM((64, 128), F32),
            pltpu.VMEM((128, NT_LOC), F32),
            pltpu.VMEM((128, 128), F32),
            pltpu.VMEM((NT_LOC, 256), BF16),
            pltpu.VMEM((NT_LOC, 256), BF16),
            pltpu.VMEM((NR, 8, NT_LOC), F32),
            pltpu.VMEM((NR - 1, 8, NT_LOC), F32),
            pltpu.VMEM((NR - 1, 16, 128), F32),
            pltpu.VMEM((NR, 8, NT_LOC), F32),
            pltpu.VMEM((NR, 64, 128), F32),
            pltpu.VMEM((32, 128), F32),
            pltpu.VMEM((7, 16, 128), F32),
            pltpu.VMEM((32, 128), F32),
            pltpu.VMEM((32, 128), F32),
            pltpu.VMEM((32, 128), F32),
            pltpu.VMEM((32, 128), F32),
            pltpu.VMEM((32, 128), F32),
            pltpu.VMEM((RANK, CH), F32),
            pltpu.VMEM((64, RANK), F32),
            dma, dma, dma,
            dma((2,)), dma((2,)), dma((2,)), dma((2,)), dma((2,)), dma((2, 7)), dma((2,)), dma((2, 4)),
            dma, dma, dma, dma, dma, dma, dma, dma,
            dma, dma, dma, dma, dma, dma, dma, dma,
        ],
        compiler_params=pltpu.CompilerParams(
            collective_id=0, has_side_effects=True, vmem_limit_bytes=FACTOR_VMEM * 1024 * 1024
        ),
        cost_estimate=pl.CostEstimate(flops=13_000_000_000, bytes_accessed=12_000_000, transcendentals=0),
        name="factor_updates",
    )(observed, ut, v)


def slabs_kernel(obs_ref, us_ref, vs_ref, u_ref, v_ref, low_ref, sparse_ref, u_out, v_out):
    def low(k):
        us = us_ref[k]
        return dot(jnp.concatenate([us, us], axis=1), vs_ref[k])

    low_ref[...] = low(0)
    diff = obs_ref[...] - low(1)
    sparse_ref[...] = diff - jnp.clip(diff, -SHRINK, SHRINK)
    u_out[...] = u_ref[...]
    v_out[...] = v_ref[...]


def slabs(observed, ust, vst, u, v):
    block = 512
    wide = pl.BlockSpec((block, NT_LOC), lambda i: (i, 0))
    u_spec = pl.BlockSpec((RANK, CH), lambda i: (0, 0))
    v_spec = pl.BlockSpec((64, RANK), lambda i: (0, 0))
    slab = jax.ShapeDtypeStruct((NS_LOC, NT_LOC), F32)
    return pl.pallas_call(
        slabs_kernel,
        grid=(NS_LOC // block,),
        out_shape=(slab, slab, jax.ShapeDtypeStruct((RANK, CH), F32), jax.ShapeDtypeStruct((64, RANK), F32)),
        in_specs=[
            wide,
            pl.BlockSpec((2, block, 128), lambda i: (0, i, 0)),
            pl.BlockSpec((2, 256, NT_LOC), lambda i: (0, 0, 0)),
            u_spec,
            v_spec,
        ],
        out_specs=(wide, wide, u_spec, v_spec),
        compiler_params=pltpu.CompilerParams(vmem_limit_bytes=SLABS_VMEM * 1024 * 1024),
        name="final_slabs",
    )(observed, ust, vst, u, v)


def shards(observed, u_start, v_start):
    ust, vst, ut, v_own = factors(observed, u_start.T, v_start)
    low, sparse, ut, v_own = slabs(observed, ust, vst, ut, v_own)
    return (low, sparse, ut.T, v_own)


def solution(mesh):
    return jax.shard_map(
        shards,
        mesh=mesh,
        in_specs=(P("rows", "cols"), P(("rows", "cols"), None), P(("cols", "rows"), None)),
        out_specs=(
            P("rows", "cols"),
            P("rows", "cols"),
            P(("rows", "cols"), None),
            P(("cols", "rows"), None),
        ),
        check_vma=False,
    )
```
